128 devices in a mesh: row: 8 (over y, core), col: 16 (over x, z).
Axes of the slice: x: 4, y: 4, z: 4, core: 2. Of those that a mesh axis runs over, the one named last changes fastest.
Arguments:
- hidden_in: bfloat16 [256, 2, 6144], P(('row', 'col')), may hold values from -6 to 6
- queries: bfloat16 [256, 2, 6144], P(('row', 'col')), may hold values from -9 to 9
- new_kv: bfloat16 [256, 2, 2048], P(('row', 'col')), may hold values from -6 to 6
- kv_pool: bfloat16 [4096, 16, 2048], P(('row', 'col')), may hold values from -6 to 6
- block_table: int32 [256, 64], replicated, may hold values from -1 to 4095, as said below
- cached_len: int32 [256], replicated, may hold values from 1 to 1024, as said below
- w_out: bfloat16 [6144, 6144], P('col'), may hold values from -0.078125 to 0.078125
- norm_gain: bfloat16 [6144], replicated, may hold values from 0.5 to 1.5
- expert_ids: int32 [256, 2, 2], P(('row', 'col')), may hold values from 0 to 7, all different within a row; in each aligned block of 4 rows (0 to 3, 4 to 7, ..., all dimensions but the last counted through in order) at most 3 rows name the same one
- expert_gates: float32 [256, 2, 2], P(('row', 'col')), may hold values from 0.2 to 1
- w_gate: bfloat16 [8, 6144, 8192], P('row', None, 'col'), may hold values from -0.078125 to 0.078125
- w_up: bfloat16 [8, 6144, 8192], P('row', None, 'col'), may hold values from -0.078125 to 0.078125
- w_down: bfloat16 [8, 8192, 6144], P('row', 'col'), may hold values from -0.0625 to 0.0625
Outputs:
- layer_out: bfloat16 [256, 2, 6144], P(('row', 'col'))
The draws below stay inside these ranges and needn't reach their ends.
Inputs may be any that keep to these rules, and one draw needn't show every extreme that they name: `block_table`: row i lists request i's blocks in order for b < ceil(cached_len[i] / 16) and -1 after; no block is listed twice; the blocks of device d are rows d * 32 to d * 32 + 31 of kv_pool; in every draw all 32 blocks of some device are listed. `cached_len`: some request has exactly 1024 cached positions. `expert_ids`: the two experts of a token-step differ; among the 4 token-steps of one device (aligned blocks of rows in request-major order) no expert is named more than 3 times.
All inputs are finite; a program needn't handle non-finite values.
Results may differ from the reference program's by a relative error of at most 0.018.
Values may be sent and summed in bfloat16 or wider, within the bound.
A program may use at most 192 MiB of HBM per device.

```python
import math
import jax
import jax.numpy as jnp
import numpy as np
from jax import lax

D = 6144
HEADS = 48
KVH = 8
HD = 128
EXPERTS = 8
FF = 8192
TOPK = 2
STEPS = 2
BS = 16
MAXBLK = 64
CAP = 3
NBLK = 32
REQS = 256
TOK_DEV = 4
POOL_BLOCKS = 4096


def cache_layout(key):
    keys = jax.random.split(key, 8)
    factor_one = jax.random.randint(keys[0], (REQS,), 0, 64)
    factor_two = jax.random.randint(keys[1], (REQS,), 0, 64)
    factor_three = jax.random.randint(keys[2], (REQS,), 0, 64)
    extra = factor_one * factor_two * factor_three * (MAXBLK - 1) // (64 * 64 * 64)
    longest = jax.random.randint(keys[3], (), 0, REQS)
    ident = jnp.arange(REQS, dtype=jnp.int32)
    extra = jnp.where(ident == longest, MAXBLK - 1, extra)
    order_key = (ident - longest) % REQS
    before = jnp.sum(jnp.where(order_key[None, :] < order_key[:, None], extra[None, :], 0), axis=1)
    limit = POOL_BLOCKS - REQS
    extra = jnp.minimum(extra, jnp.maximum(limit - before, 0))
    counts = 1 + extra
    tails = jax.random.randint(keys[4], (REQS,), 1, BS + 1)
    tails = jnp.where(ident == longest, BS, tails)
    lengths = (counts - 1) * BS + tails
    devices_all = POOL_BLOCKS // NBLK
    device_ids = jnp.arange(devices_all, dtype=jnp.int32)
    hotness = jax.random.randint(keys[5], (devices_all,), 0, 4) == 0
    hotness = hotness | (device_ids == jax.random.randint(keys[6], (), 0, devices_all))
    device_noise = jax.random.randint(jax.random.fold_in(keys[7], 1), (devices_all,), 0, 1024)
    slot_index = jnp.arange(POOL_BLOCKS, dtype=jnp.int32)
    slot_noise = jax.random.randint(keys[7], (POOL_BLOCKS,), 0, 1024)
    owner_device = slot_index // NBLK
    primary = jnp.where(hotness[owner_device], 2048 + device_noise[owner_device], slot_noise)
    ranking = primary * POOL_BLOCKS + slot_index
    order = jnp.argsort(-ranking).astype(jnp.int32)
    firsts = jnp.cumsum(counts) - counts
    column = jnp.arange(MAXBLK, dtype=jnp.int32)
    picked = jnp.take(order, jnp.minimum(firsts[:, None] + column[None, :], POOL_BLOCKS - 1))
    table = jnp.where(column[None, :] < counts[:, None], picked, -1)
    return (table.astype(jnp.int32), lengths.astype(jnp.int32))


def draw_block_table(key, part):
    table, lengths = cache_layout(key)
    return table


def draw_cached_len(key, part):
    table, lengths = cache_layout(key)
    return lengths


def draw_kv_pool(key, part):
    key = jax.random.fold_in(key, 5)
    shape = (POOL_BLOCKS, BS, 2, KVH, HD)
    full = jnp.clip(jax.random.normal(key, shape, jnp.float32), -6.0, 6.0)
    return full.reshape(POOL_BLOCKS, BS, 2 * KVH * HD).astype(jnp.bfloat16)


def draw_queries(key, part):
    key = jax.random.fold_in(key, 9)
    groups = HEADS // KVH
    shape = (REQS, STEPS, KVH, groups, HD)
    first = jax.random.fold_in(key, 0)
    full = jnp.clip(jax.random.normal(first, shape, jnp.float32), -6.0, 6.0)
    return full.reshape(REQS, STEPS, HEADS * HD).astype(jnp.bfloat16)


def levels(stream_key, dims, shards, least, high):
    factor_of, own = 1.0, jax.random.fold_in(stream_key, 6)
    for position, blocks in shards:
        draws = jnp.exp(jax.random.uniform(jax.random.fold_in(own, position), (blocks,), jnp.float32, least / len(shards), high / len(shards)))
        factor_of = factor_of * jnp.repeat(draws, dims[position] // blocks).reshape([-1 if axis == position else 1 for axis in range(len(dims))])
    return factor_of


def shared_out(rng, own, number, rows, count, top, reach, lean):
    order = jax.random.permutation(rng, count)
    packed, usual = load_shares(count, rows * top, reach, lean, True), load_shares(count, rows * top, reach, lean, False)
    places = jnp.arange(count)

    def named(sizes, turn):
        used = int((sizes > 0).sum())
        fixed = max(1, used // 4)
        passed = fixed + (places - fixed + turn * (used - fixed)) % max(1, count - fixed)
        return jnp.zeros((count,), jnp.int32).at[order[jnp.where(places < fixed, places, passed)]].set(jnp.asarray(sizes, jnp.int32))

    sizes = jnp.where(number % 4 == 0, named(packed, number // 4), named(usual, number - number // 4 - 1))
    mixed = jax.random.permutation(jax.random.fold_in(own, 3), count)
    source_of, taker = mixed[0:count // 2 * 2:2], mixed[1:count // 2 * 2:2]
    room = jnp.minimum(sizes[source_of] - 1, reach - sizes[taker]) // 2
    room = jnp.where((source_of == order[0]) | (taker == order[0]) | (sizes[taker] == 0), 0, jnp.maximum(room, 0))
    passed = jax.random.randint(jax.random.fold_in(own, 4), (count // 2,), 0, 1 << 20) % (room + 1)
    sizes = sizes.at[source_of].add(-passed).at[taker].add(passed)
    members = jnp.searchsorted(jnp.cumsum(sizes), jnp.arange(rows * top), side="right").astype(jnp.int32)
    table = members.reshape(top, rows).T
    table = table[jax.random.permutation(jax.random.fold_in(own, 1), rows)]
    turn = jax.random.randint(jax.random.fold_in(own, 2), (rows, 1), 0, top)
    return jnp.take_along_axis(table, (jnp.arange(top)[None, :] + turn) % top, axis=1)


def load_shares(number_of, total, most, slope, full):
    weights = [(1 << 20) // math.isqrt(grade ** slope) + 1 for grade in range(1, number_of + 1)]
    largest = most if full else min(most, max(-(-total // number_of), total * weights[0] // sum(weights)))
    least = 1 if total - largest >= number_of - 1 else 0
    given, surplus = [largest] + [least] * (number_of - 1), total - largest - least * (number_of - 1)
    while surplus > 0:
        candidates = [i for i in range(1, number_of) if given[i] < largest] or [i for i in range(1, number_of) if given[i] < most]
        mass, budget = sum([weights[i] for i in candidates]), surplus
        for i in candidates:
            addition = min(most - given[i], max(1, budget * weights[i] // mass), surplus)
            given[i] = given[i] + addition
            surplus = surplus - addition
    return np.array(given)


def centred(stream_key, extent, scale, reach, cuts=(), kind=jnp.bfloat16):
    loudness = levels(stream_key, extent, cuts, -0.22, 0.18) if cuts else 1.0
    result = jax.random.normal(stream_key, extent, jnp.float32) * scale * loudness
    return jnp.minimum(jnp.maximum(result, -reach), reach).astype(kind)


def setup_inputs(seed: int = 0) -> dict:
    seeds = jax.random.split(jax.random.key(seed), 14)
    hidden_in = centred(seeds[0], (REQS, STEPS, D), 1.0, 6.0, ((0, 128),))
    queries = draw_queries(jax.random.fold_in(seeds[13], 71), 0)
    new_kv = centred(seeds[2], (REQS, STEPS, 2 * KVH * HD), 1.0, 6.0, ((0, 128),))
    kv_pool = draw_kv_pool(jax.random.fold_in(seeds[13], 71), 0)
    block_table = draw_block_table(jax.random.fold_in(seeds[13], 71), 0)
    cached_len = draw_cached_len(jax.random.fold_in(seeds[13], 71), 0)
    w_out = centred(seeds[6], (D, D), D ** -0.5, 0.078125, ((0, 16),))
    norm_gain = jnp.clip(1.0 + 0.1 * jax.random.normal(seeds[7], (D,), jnp.float32), 0.5, 1.5).astype(jnp.bfloat16)
    expert_ids_keys = jax.random.split(jax.random.fold_in(seeds[8], 1), REQS * STEPS // TOK_DEV)
    expert_ids_turns = jax.random.permutation(jax.random.fold_in(seeds[8], 3), REQS * STEPS // TOK_DEV)
    expert_ids = jax.vmap(lambda own, number: shared_out(jax.random.fold_in(seeds[8], 2), own, number, TOK_DEV, EXPERTS, TOPK, CAP, 2))(expert_ids_keys, expert_ids_turns).reshape((REQS, STEPS, TOPK))
    expert_gates = jnp.clip(0.2 + 0.8 * jax.random.uniform(seeds[9], (REQS, STEPS, TOPK), jnp.float32) ** levels(seeds[9], (REQS, STEPS, TOPK), ((0, 128),), -0.2, 0.2), 0.2, 1.0)
    w_gate = centred(seeds[10], (EXPERTS, D, FF), D ** -0.5, 0.078125, ((0, 8), (2, 16)))
    w_up = centred(seeds[11], (EXPERTS, D, FF), D ** -0.5, 0.078125, ((0, 8), (2, 16)))
    w_down = centred(seeds[12], (EXPERTS, FF, D), FF ** -0.5, 0.0625, ((0, 8), (1, 16)))
    return {"hidden_in": hidden_in, "queries": queries, "new_kv": new_kv, "kv_pool": kv_pool, "block_table": block_table, "cached_len": cached_len, "w_out": w_out, "norm_gain": norm_gain, "expert_ids": expert_ids, "expert_gates": expert_gates, "w_gate": w_gate, "w_up": w_up, "w_down": w_down}


floor_score = -1e+30

def attend_request(inputs, kv_pool):
    query, fresh, table_row, length = inputs
    groups = HEADS // KVH
    scale = HD ** (-0.5)
    blocks = kv_pool[jnp.maximum(table_row, 0)].astype(jnp.float32)
    cache = blocks.reshape(MAXBLK * BS, 2, KVH, HD)
    grouped = query.astype(jnp.float32).reshape(STEPS, KVH, groups, HD)
    newest = fresh.astype(jnp.float32).reshape(STEPS, 2, KVH, HD)
    cached_scores = jnp.einsum('skgd,tkd->skgt', grouped, cache[:, 0], precision=lax.Precision.HIGHEST) * scale
    visible = jnp.arange(MAXBLK * BS, dtype=jnp.int32) < length
    cached_scores = jnp.where(visible[None, None, None, :], cached_scores, floor_score)
    fresh_scores = jnp.einsum('skgd,ukd->skgu', grouped, newest[:, 0], precision=lax.Precision.HIGHEST) * scale
    causal = jnp.arange(STEPS)[None, :] <= jnp.arange(STEPS)[:, None]
    fresh_scores = jnp.where(causal[:, None, None, :], fresh_scores, floor_score)
    scores = jnp.concatenate([cached_scores, fresh_scores], axis=3)
    highest_score = lax.optimization_barrier(jnp.max(scores, axis=3, keepdims=True))
    weights = jnp.exp(scores - highest_score)
    totals = lax.optimization_barrier(jnp.sum(weights, axis=3))
    values = jnp.concatenate([cache[:, 1], newest[:, 1]], axis=0)
    mixed = jnp.einsum('skgt,tkd->skgd', weights, values, precision=lax.Precision.HIGHEST) / totals[..., None]
    return mixed.reshape(STEPS, HEADS * HD).astype(jnp.bfloat16)

def reference(hidden_in, queries, new_kv, kv_pool, block_table, cached_len, w_out, norm_gain, expert_ids, expert_gates, w_gate, w_up, w_down):
    attended = lax.map(lambda inputs: attend_request(inputs, kv_pool), (queries, new_kv, block_table, cached_len))
    tokens = REQS * STEPS
    flat_attended = attended.reshape(tokens, D)
    projected = jnp.dot(flat_attended, w_out, preferred_element_type=jnp.float32)
    residual = (hidden_in.reshape(tokens, D).astype(jnp.float32) + projected).astype(jnp.bfloat16)
    stream = residual.astype(jnp.float32)
    normed = (stream * lax.rsqrt(lax.optimization_barrier(jnp.mean(stream * stream, axis=1, keepdims=True)) + 1e-05) * norm_gain.astype(jnp.float32)).astype(jnp.bfloat16)
    picks = expert_ids.reshape(tokens, TOPK)
    gates = expert_gates.reshape(tokens, TOPK)
    chosen = (picks[:, :, None] == jnp.arange(EXPERTS, dtype=jnp.int32)[None, None, :]).astype(jnp.float32)
    combine = lax.optimization_barrier(jnp.sum(chosen * gates[:, :, None], axis=1))

    def expert_step(total, inputs):
        gate_matrix, up_matrix, down_matrix, weight_column = inputs
        gated = jnp.dot(normed, gate_matrix, preferred_element_type=jnp.float32)
        upward = jnp.dot(normed, up_matrix, preferred_element_type=jnp.float32)
        active = (jax.nn.silu(gated) * upward).astype(jnp.bfloat16)
        output = jnp.dot(active, down_matrix, preferred_element_type=jnp.float32).astype(jnp.bfloat16)
        return (total + weight_column[:, None] * output.astype(jnp.float32), None)
    mixture, unused = lax.scan(expert_step, jnp.zeros((tokens, D), jnp.float32), (w_gate, w_up, w_down, combine.T))
    return (stream + mixture).astype(jnp.bfloat16).reshape(REQS, STEPS, D)
```

```python
import jax, functools
import jax.numpy as jnp
from jax import lax
from jax.experimental import pallas as pl
from jax.experimental.pallas import tpu as pltpu
from jax.sharding import PartitionSpec as P

MESH = pl.DeviceIdType.MESH
ORDERS = (("x", "y", "z"), ("y", "z", "x"), ("z", "x", "y"))
F32, BF16 = jnp.float32, jnp.bfloat16


def where_am_i():
    r, c = lax.axis_index("row"), lax.axis_index("col")
    return {"y": r // 2, "k": r % 2, "x": c // 4, "z": c % 4}


def device(me, **moved):
    at = dict(me)
    for name, step in moved.items():
        at[name] = (me[name] + step) % (2 if name == "k" else 4)
    return (at["y"] * 2 + at["k"], at["x"] * 4 + at["z"])


def pick(sel, name):
    return sel.get(name, slice(None))


def block_of(ref, k, sel, part):
    return ref.at[(pick(sel, "y"), k, pick(sel, "x"), pick(sel, "z")) + part]


def remote(src, dst, send, recv, where):
    return pltpu.make_async_remote_copy(
        src_ref=src, dst_ref=dst, send_sem=send, recv_sem=recv, device_id=where, device_id_type=MESH
    )


def greet(me, plane=False):
    bar = pltpu.get_barrier_semaphore()
    count = 0
    for name in ("x", "y", "z"):
        for d in (1, 2, 3):
            pl.semaphore_signal(bar, inc=1, device_id=device(me, **{name: d}), device_id_type=MESH)
            count += 1
    pl.semaphore_signal(bar, inc=1, device_id=device(me, k=1), device_id_type=MESH)
    count += 1
    if plane:
        for dx in (1, 2, 3):
            for dz in (1, 2, 3):
                pl.semaphore_signal(bar, inc=1, device_id=device(me, x=dx, z=dz), device_id_type=MESH)
                count += 1
    pl.semaphore_wait(bar, count)


def shift(me, **moved):
    return {n: (me[n] - s) % 4 for n, s in moved.items()}


def gather_blocks(buf, me, parts, send, recv, cs, cr):
    k = me["k"]
    started = []

    def go(p, sel, moved, i):
        there = block_of(buf, k, sel, parts[p])
        copy = remote(there, there, send.at[p, i], recv.at[p, i], device(me, **moved))
        copy.start()
        started.append(copy)

    def landed(p, sel, i):
        here = block_of(buf, k, sel, parts[p])
        remote(here, here, send.at[p, i], recv.at[p, i], device(me, k=1)).wait_recv()

    def across(p, sel, i):
        there = block_of(buf, k, sel, parts[p])
        copy = remote(there, there, cs.at[p, i], cr.at[p, i], device(me, k=1))
        copy.start()
        started.append(copy)

    for p, (a, b, c) in enumerate(ORDERS):
        for d in (2, 1, 3):
            go(p, {n: me[n] for n in "xyz"}, {a: d}, d - 1)
    for p, (a, b, c) in enumerate(ORDERS):
        for d in (1, 3, 2):
            landed(p, {a: (me[a] - d) % 4, b: me[b], c: me[c]}, d - 1)
        line = {b: me[b], c: me[c]}
        for d in (2, 1, 3):
            go(p, line, {b: d}, 3 + d - 1)
        for d in (2, 1, 3):
            go(p, line, {c: d}, 6 + d - 1)
        across(p, line, 0)
    for d in (1, 3, 2):
        for p, (a, b, c) in enumerate(ORDERS):
            line = {b: (me[b] - d) % 4, c: me[c]}
            landed(p, line, 3 + d - 1)
            for e in (2, 1, 3):
                go(p, line, {c: e}, 9 + (d - 1) * 3 + e - 1)
            across(p, line, d)
    for e in (1, 3, 2):
        for p, (a, b, c) in enumerate(ORDERS):
            landed(p, {b: me[b], c: (me[c] - e) % 4}, 6 + e - 1)
            for d in (1, 3, 2):
                landed(p, {b: (me[b] - d) % 4, c: (me[c] - e) % 4}, 9 + (d - 1) * 3 + e - 1)
            across(p, {c: (me[c] - e) % 4}, 3 + e)
    other = 1 - k
    for p, (a, b, c) in enumerate(ORDERS):
        for i, sel in enumerate(
            [{b: me[b], c: me[c]}]
            + [{b: (me[b] - d) % 4, c: me[c]} for d in (1, 2, 3)]
            + [{c: (me[c] - e) % 4} for e in (1, 2, 3)]
        ):
            here = block_of(buf, other, sel, parts[p])
            remote(here, here, cs.at[p, i], cr.at[p, i], device(me, k=1)).wait_recv()
    for copy in started:
        copy.wait_send()


def send_core(buf, me, parts, core, cs, cr, p):
    copy = remote(
        buf.at[(slice(None), 1 - me["k"], slice(None), slice(None)) + parts[p]],
        core.at[(slice(None), slice(None), slice(None)) + parts[p]],
        cs.at[p], cr.at[p], device(me, k=1),
    )
    copy.start()
    return copy


def scatter_blocks(buf, me, parts, core, r1, r2, r3, send, recv, started):
    k = me["k"]

    def go(p, sel, moved, dst, i):
        copy = remote(block_of(buf, k, sel, parts[p]), dst, send.at[p, i], recv.at[p, i], device(me, **moved))
        copy.start()
        started.append(copy)

    def landed(p, dst, i):
        remote(dst, dst, send.at[p, i], recv.at[p, i], device(me, k=1)).wait_recv()

    def add_core(p, c, at):
        rest = [n for n in ("y", "x", "z") if n != c]

        def body(i, _):
            idx = {c: at, rest[0]: i // 4, rest[1]: i % 4}
            mine = (idx["y"], k, idx["x"], idx["z"]) + parts[p]
            theirs = (idx["y"], idx["x"], idx["z"]) + parts[p]
            buf[mine] = (buf[mine].astype(F32) + core[theirs].astype(F32)).astype(BF16)
            return 0

        lax.fori_loop(0, 16, body, 0)

    for p, (a, b, c) in enumerate(ORDERS):
        started[p].wait_recv()
        for d in (2, 1, 3):
            add_core(p, c, (me[c] + d) % 4)
            go(p, {c: (me[c] + d) % 4}, {c: d}, r1.at[p, d - 1], d - 1)
    for p, (a, b, c) in enumerate(ORDERS):
        add_core(p, c, me[c])
    for p, (a, b, c) in enumerate(ORDERS):
        for d in (1, 2, 3):
            landed(p, r1.at[p, d - 1], d - 1)
        rest = [n for n in ("y", "x", "z") if n != c]

        def body(i, _):
            idx = {c: me[c], rest[0]: i // 4, rest[1]: i % 4}
            mine = (idx["y"], k, idx["x"], idx["z"]) + parts[p]
            total = buf[mine].astype(F32)
            for d in range(3):
                total += r1[p, d, i // 4, i % 4].astype(F32)
            buf[mine] = total.astype(BF16)
            return 0

        lax.fori_loop(0, 16, body, 0)
        for d in (2, 1, 3):
            go(p, {c: me[c], b: (me[b] + d) % 4}, {b: d}, r2.at[p, d - 1], 3 + d - 1)
    for p, (a, b, c) in enumerate(ORDERS):
        for d in (1, 2, 3):
            landed(p, r2.at[p, d - 1], 3 + d - 1)
        for i in range(4):
            idx = {c: me[c], b: me[b], a: i}
            mine = (idx["y"], k, idx["x"], idx["z"]) + parts[p]
            total = buf[mine].astype(F32)
            for d in range(3):
                total += r2[p, d, i].astype(F32)
            buf[mine] = total.astype(BF16)
        for d in (2, 1, 3):
            go(p, {c: me[c], b: me[b], a: (me[a] + d) % 4}, {a: d}, r3.at[p, d - 1], 6 + d - 1)
    sums = []
    for p, (a, b, c) in enumerate(ORDERS):
        for d in (1, 2, 3):
            landed(p, r3.at[p, d - 1], 6 + d - 1)
        total = buf[(me["y"], k, me["x"], me["z"]) + parts[p]].astype(F32)
        for d in range(3):
            total += r3[p, d].astype(F32)
        sums.append(total)
    for copy in started:
        copy.wait_send()
    return sums


def lane_parts(n):
    w = n // 3
    return [(slice(None), slice(w * p, w * p + w)) for p in range(3)]


def gather_call(block, cid):
    rows, lanes = block.shape

    def kernel(x_ref, o_ref, buf, send, recv, cs, cr, ls):
        me = where_am_i()
        greet(me)
        buf[me["y"], me["k"], me["x"], me["z"]] = x_ref[...]
        gather_blocks(buf, me, lane_parts(lanes), send, recv, cs, cr)
        cp = pltpu.make_async_copy(buf, o_ref, ls)
        cp.start()
        cp.wait()

    return pl.pallas_call(
        kernel,
        out_shape=jax.ShapeDtypeStruct((4, 2, 4, 4, rows, lanes), block.dtype),
        in_specs=[pl.BlockSpec(memory_space=pltpu.VMEM)],
        out_specs=pl.BlockSpec(memory_space=pl.ANY),
        scratch_shapes=[
            pltpu.VMEM((4, 2, 4, 4, rows, lanes), block.dtype),
            pltpu.SemaphoreType.DMA((3, 18)), pltpu.SemaphoreType.DMA((3, 18)),
            pltpu.SemaphoreType.DMA((3, 7)), pltpu.SemaphoreType.DMA((3, 7)),
            pltpu.SemaphoreType.DMA,
        ],
        compiler_params=pltpu.CompilerParams(collective_id=cid, has_side_effects=True, vmem_limit_bytes=40 * 2**20),
    )(block)


def scatter_call(blocks, cid):
    rows, lanes = blocks.shape[-2:]
    w = lanes // 3

    def kernel(x_ref, o_ref, buf, core, r1, r2, r3, send, recv, cs, cr, ls):
        me = where_am_i()
        cp = pltpu.make_async_copy(x_ref, buf, ls)
        cp.start()
        greet(me)
        cp.wait()
        started = [send_core(buf, me, lane_parts(lanes), core, cs, cr, p) for p in range(3)]
        sums = scatter_blocks(buf, me, lane_parts(lanes), core, r1, r2, r3, send, recv, started)
        for p in range(3):
            o_ref[:, w * p : w * p + w] = sums[p]

    return pl.pallas_call(
        kernel,
        out_shape=jax.ShapeDtypeStruct((rows, lanes), F32),
        in_specs=[pl.BlockSpec(memory_space=pl.ANY)],
        out_specs=pl.BlockSpec(memory_space=pltpu.VMEM),
        scratch_shapes=[
            pltpu.VMEM((4, 2, 4, 4, rows, lanes), BF16),
            pltpu.VMEM((4, 4, 4, rows, lanes), BF16),
            pltpu.VMEM((3, 3, 4, 4, rows, w), BF16),
            pltpu.VMEM((3, 3, 4, rows, w), BF16),
            pltpu.VMEM((3, 3, rows, w), BF16),
            pltpu.SemaphoreType.DMA((3, 9)), pltpu.SemaphoreType.DMA((3, 9)),
            pltpu.SemaphoreType.DMA((3,)), pltpu.SemaphoreType.DMA((3,)),
            pltpu.SemaphoreType.DMA,
        ],
        compiler_params=pltpu.CompilerParams(collective_id=cid, has_side_effects=True, vmem_limit_bytes=40 * 2**20),
    )(blocks)


ANY = pl.BlockSpec(memory_space=pl.ANY)
VM = pl.BlockSpec(memory_space=pltpu.VMEM)
DMA = pltpu.SemaphoreType.DMA
XPARTS = [(slice(None), slice(0, 512)), (slice(None), slice(512, 1024)), (slice(None), slice(1024, 1664))]


def experts_kernel(xb, rb, wg_h, wu_h, wd_h, o_ref, X, WG, WU, WD, S, core, r1, r2, r3, accg, accu, act, scal, fout, fin,
                   wsem, gs, gr, gcs, gcr, ss_, sr, scs, scr, fs, fr):
    me = where_am_i()
    k = me["k"]
    loads = [pltpu.make_async_copy(h, v, wsem.at[i]) for i, (h, v) in enumerate(((wg_h, WG), (wu_h, WU), (wd_h, WD)))]
    for c in loads:
        c.start()
    greet(me)
    X[me["y"], k, me["x"], me["z"]] = xb[...]
    gather_blocks(X, me, XPARTS, gs, gr, gcs, gcr)
    loads[0].wait()
    loads[1].wait()
    parts = lane_parts(1536)
    expert = me["y"] * 2 + k
    started = []
    for half in range(2):
        kk = 1 - k if half == 0 else k
        extra = jnp.zeros((256, 128), F32)
        for z in range(4):
            extra += X[:, kk, :, z, :, 1536:1664].reshape(256, 128).astype(F32)
        lane = lax.broadcasted_iota(jnp.int32, (256, 128), 1)
        squares = jnp.sum(jnp.where(lane < 3, extra, 0.0), axis=1, keepdims=True)
        weight = jnp.sum(jnp.where((lane == 8 + expert) | (lane == 16 + expert), extra, 0.0), axis=1, keepdims=True)
        rs = lax.rsqrt(squares * (1.0 / 6144.0) + 1e-5)
        scal[0] = jnp.broadcast_to(rs, (256, 128))
        scal[1] = jnp.broadcast_to(weight, (256, 128))

        def body(z, _):
            rows = pl.ds(pl.multiple_of(z * 1536, 1536), 1536)
            x = X[:, kk, :, z, :, 0:1536].reshape(256, 1536)
            for n in range(2):
                cols = slice(256 * n, 256 * n + 256)
                g = jnp.dot(x, WG[rows, cols], preferred_element_type=F32)
                u = jnp.dot(x, WU[rows, cols], preferred_element_type=F32)
                keep = jnp.where(z == 0, 0.0, 1.0)
                accg[:, cols] = accg[:, cols] * keep + g
                accu[:, cols] = accu[:, cols] * keep + u
            return 0

        accg[...] = jnp.zeros_like(accg)
        accu[...] = jnp.zeros_like(accu)
        lax.fori_loop(0, 4, body, 0)
        rs = scal[0, :, 0:1]
        weight = scal[1, :, 0:1]
        g = accg[...] * rs
        act[...] = (g / (1.0 + jnp.exp(-g)) * (accu[...] * rs) * weight).astype(BF16)
        if half == 0:
            loads[2].wait()
        for p in range(3):
            def down(z, _):
                cols = pl.ds(pl.multiple_of(z * 1536 + 512 * p, 512), 512)
                r = jnp.dot(act[...], WD[:, cols], preferred_element_type=F32)
                S[:, kk, :, z, :, 512 * p : 512 * p + 512] = r.astype(BF16).reshape(4, 4, 16, 512)
                return 0

            lax.fori_loop(0, 4, down, 0)
            if half == 0:
                started.append(send_core(S, me, parts, core, scs, scr, p))
    sums = scatter_blocks(S, me, parts, core, r1, r2, r3, ss_, sr, started)
    total = jnp.concatenate(sums, axis=1) + rb[...].astype(F32)
    for z in range(4):
        rows = total[4 * z : 4 * z + 4]
        fout[z] = jnp.concatenate([rows[:, 384 * q : 384 * q + 384] for q in range(4)], axis=0).astype(BF16)
    outs = []
    for d in (2, 1, 3):
        c = remote(fout.at[(me["z"] + d) % 4], fin.at[me["z"]], fs.at[d - 1], fr.at[d - 1], device(me, z=d))
        c.start()
        outs.append(c)
    fin[me["z"]] = fout[me["z"]]
    for d in (1, 3, 2):
        there = fin.at[(me["z"] - d) % 4]
        remote(there, there, fs.at[d - 1], fr.at[d - 1], device(me, k=1)).wait_recv()
    for c in outs:
        c.wait_send()
    o_ref[...] = fin[...]


def experts_call(xb, rb, wg, wu, wd, cid):
    V = pltpu.VMEM
    return pl.pallas_call(
        experts_kernel,
        out_shape=jax.ShapeDtypeStruct((4, 16, 384), BF16),
        in_specs=[VM, VM, ANY, ANY, ANY],
        out_specs=VM,
        scratch_shapes=[
            V((4, 2, 4, 4, 16, 1664), BF16), V((6144, 512), BF16), V((6144, 512), BF16), V((512, 6144), BF16),
            V((4, 2, 4, 4, 16, 1536), BF16), V((4, 4, 4, 16, 1536), BF16),
            V((3, 3, 4, 4, 16, 512), BF16), V((3, 3, 4, 16, 512), BF16), V((3, 3, 16, 512), BF16),
            V((256, 512), F32), V((256, 512), F32), V((256, 512), BF16), V((2, 256, 128), F32),
            V((4, 16, 384), BF16), V((4, 16, 384), BF16),
            DMA((3,)), DMA((3, 18)), DMA((3, 18)), DMA((3, 7)), DMA((3, 7)), DMA((3, 9)), DMA((3, 9)), DMA((3,)), DMA((3,)),
            DMA((3,)), DMA((3,)),
        ],
        compiler_params=pltpu.CompilerParams(collective_id=cid, has_side_effects=True, vmem_limit_bytes=60 * 2**20),
    )(xb, rb, wg, wu, wd)


QPARTS = [(slice(64 * p, 64 * p + 64), slice(None)) for p in range(3)]
EMPTY = 34


def attend_kernel(req, seen, prev, last, qb, nk, nvt, hin, gain, gtile, kv_h, wo_h, xb_o, rb_o,
                  Q, A, KV, VT, WO, accs, ms, ls, Z, Zm, Zl, St, Cst, core, r1, r2, r3, s1, St2, s2, St3, s3, Wt,
                  U, G, H, O, Rv, hid, hrec,
                  lsem, gs, gr, gcs, gcr, ss_, sr, ts, tr, scs, scr, tcs, tcr, hs, hr, as_, ar, ps, pr):
    me = where_am_i()
    k = me["k"]
    kv_load = pltpu.make_async_copy(kv_h, KV, lsem.at[0])
    wo_load = pltpu.make_async_copy(wo_h, WO, lsem.at[1])
    kv_load.start()
    wo_load.start()
    greet(me, plane=True)
    started = []
    Q[me["y"], k, me["x"], me["z"]] = qb[...]
    gather_blocks(Q, me, QPARTS, gs, gr, gcs, gcr)
    for d in (1, 2, 3):
        c = remote(hin.at[(me["z"] + d) % 4], hrec.at[me["z"]], hs.at[d - 1], hr.at[d - 1], device(me, z=d))
        c.start()
        started.append(c)
    hrec[me["z"]] = hin[me["z"]]
    kv_load.wait()

    def turn(j, _):
        v = jnp.concatenate([KV[j, :, 1024 + 128 * g : 1152 + 128 * g] for g in range(8)], axis=0)
        VT[j] = v.astype(F32).T.astype(BF16)
        return 0

    lax.fori_loop(0, 32, turn, 0)

    lane = lax.broadcasted_iota(jnp.int32, (128, 192), 1)
    rowi = lax.broadcasted_iota(jnp.int32, (128, 192), 0)
    head_kv = ((lane // 64) * 16 + lane % 16) // 6
    lane_i = (lane // 32) % 2
    lane_s = (lane // 16) % 2
    same = jnp.where(head_kv == rowi // 16, rowi % 16, 99)

    def slot(j, _):
        rq = req[j]
        q = Q[rq // 64, (rq // 32) % 2, (rq // 8) % 4, (rq // 2) % 4]
        ks = jnp.concatenate([KV[j, :, 128 * g : 128 * g + 128] for g in range(8)], axis=0)
        st = lax.dot_general(ks, q, (((1,), (1,)), ((), ())), preferred_element_type=F32) * (128 ** -0.5)
        st = jnp.where((same < seen[j]) & (lane_i == rq % 2), st, -1e30)
        m = jnp.max(st, axis=0, keepdims=True)
        w = jnp.exp(st - m)
        accs[j] = jnp.dot(VT[j], w.astype(BF16), preferred_element_type=F32)
        ms[j] = m
        ls[j] = jnp.sum(w, axis=0, keepdims=True)
        return 0

    lax.fori_loop(0, 32, slot, 0)
    own = Q[me["y"], k, me["x"], me["z"]]
    for i in range(2):
        st = lax.dot_general(nk[i], own, (((1,), (1,)), ((), ())), preferred_element_type=F32) * (128 ** -0.5)
        r = rowi[:16]
        ok = (head_kv[:16] == r // 2) & (r % 2 <= lane_s[:16]) & (lane_i[:16] == i)
        st = jnp.where(ok, st, -1e30)
        m = jnp.max(st, axis=0, keepdims=True)
        w = jnp.exp(st - m)
        accs[32 + i] = jnp.dot(nvt[i], w.astype(BF16), preferred_element_type=F32)
        ms[32 + i] = m
        ls[32 + i] = jnp.sum(w, axis=0, keepdims=True)
        accs[EMPTY + i] = jnp.zeros((128, 192), F32)
        ms[EMPTY + i] = jnp.full((1, 192), -1e30, F32)
        ls[EMPTY + i] = jnp.zeros((1, 192), F32)

    def chain(j, _):
        pj = prev[j]
        i = req[j] % 2
        m0, m1 = ms[j], ms[pj]
        m = jnp.maximum(m0, m1)
        w0, w1 = jnp.exp(m0 - m), jnp.exp(m1 - m)
        acc = accs[j] * w0 + accs[pj] * w1
        l = ls[j] * w0 + ls[pj] * w1
        accs[j] = acc
        ms[j] = m
        ls[j] = l
        mine = lane_i == i
        acc = jnp.where(mine, acc, 0.0)
        m = jnp.where(mine[:1], m, 0.0)
        l = jnp.where(mine[:1], l, 0.0)
        for p in range(3):
            s = slice(64 * p, 64 * p + 64)
            Z[j, p] = jnp.concatenate([acc[:64, s], acc[64:, s]], axis=1).astype(BF16)
            Zm[j, p] = jnp.concatenate([m[:, s], m[:, s]], axis=1)
            Zl[j, p] = jnp.concatenate([l[:, s], l[:, s]], axis=1)
        return 0

    lax.fori_loop(0, 36, chain, 0)

    def spread(kk):
        def body(n, _):
            y, x, z = n // 16, (n // 4) % 4, n % 4
            rank = y * 32 + kk * 16 + x * 4 + z
            s0, s1_ = last[2 * rank], last[2 * rank + 1]
            at = {"y": y, "x": x, "z": z}
            for p, (a, b, c) in enumerate(ORDERS):
                A[y, kk, x, z, 64 * p : 64 * p + 64, :] = Z[s0, p] + Z[s1_, p]
                row = pl.ds(at[b] * 4 + at[a], 1)
                St[p, kk, at[c], 0, row, :] = Zm[s0, p] + Zm[s1_, p]
                St[p, kk, at[c], 1, row, :] = Zl[s0, p] + Zl[s1_, p]
            return 0

        lax.fori_loop(0, 64, body, 0)

    spread(1 - k)
    cores = []
    for p in range(3):
        c0 = send_core(A, me, QPARTS, core, scs, scr, p)
        c1 = remote(St.at[p, 1 - k], Cst.at[p], tcs.at[p], tcr.at[p], device(me, k=1))
        c1.start()
        cores.append((c0, c1))
        started.extend((c0, c1))
    spread(k)

    def go(p, sel, moved, dst, i, stat, sdst):
        c0 = remote(block_of(A, k, sel, QPARTS[p]), dst, ss_.at[p, i], sr.at[p, i], device(me, **moved))
        c1 = remote(stat, sdst, ts.at[p, i], tr.at[p, i], device(me, **moved))
        c0.start()
        c1.start()
        started.extend((c0, c1))

    def landed(p, dst, i, sdst):
        remote(dst, dst, ss_.at[p, i], sr.at[p, i], device(me, k=1)).wait_recv()
        remote(sdst, sdst, ts.at[p, i], tr.at[p, i], device(me, k=1)).wait_recv()

    def merge(stats):
        top = functools.reduce(jnp.maximum, [m for m, _ in stats])
        ws = [jnp.exp(m - top) for m, _ in stats]
        return top, sum(w * l for w, (_, l) in zip(ws, stats)), ws

    def others(c):
        return [n for n in ("y", "x", "z") if n != c]

    for p, (a, b, c) in enumerate(ORDERS):
        for copy in cores[p]:
            copy.wait_recv()
        for d in (2, 1, 3, 0):
            at = (me[c] + d) % 4
            top, tot, ws = merge([(St[p, k, at, 0], St[p, k, at, 1]), (Cst[p, at, 0], Cst[p, at, 1])])
            St[p, k, at, 0] = top
            St[p, k, at, 1] = tot
            for i, w in enumerate(ws):
                Wt[i] = w

            def body(n, _, at=at, p=p, a=a, b=b, c=c):
                idx = {c: at, b: n // 4, a: n % 4}
                row = pl.ds(n, 1)
                mine = (idx["y"], k, idx["x"], idx["z"]) + QPARTS[p]
                theirs = (idx["y"], idx["x"], idx["z"]) + QPARTS[p]
                A[mine] = (A[mine].astype(F32) * Wt[0, row, :] + core[theirs].astype(F32) * Wt[1, row, :]).astype(BF16)
                return 0

            lax.fori_loop(0, 16, body, 0)
            if d:
                go(p, {c: at}, {c: d}, r1.at[p, d - 1], d - 1, St.at[p, k, at], s1.at[p, d - 1])
    for p, (a, b, c) in enumerate(ORDERS):
        for d in (1, 2, 3):
            landed(p, r1.at[p, d - 1], d - 1, s1.at[p, d - 1])
        top, tot, ws = merge([(St[p, k, me[c], 0], St[p, k, me[c], 1])] + [(s1[p, d, 0], s1[p, d, 1]) for d in range(3)])
        for i, w in enumerate(ws):
            Wt[i] = w
        for i in range(4):
            St2[p, i, 0:4] = top[4 * i : 4 * i + 4]
            St2[p, i, 4:8] = tot[4 * i : 4 * i + 4]

        def body(n, _, p=p, a=a, b=b, c=c):
            idx = {c: me[c], b: n // 4, a: n % 4}
            rest = others(c)
            row = pl.ds(n, 1)
            mine = (idx["y"], k, idx["x"], idx["z"]) + QPARTS[p]
            t = A[mine].astype(F32) * Wt[0, row, :]
            for d in range(3):
                t += r1[p, d, idx[rest[0]], idx[rest[1]]].astype(F32) * Wt[d + 1, row, :]
            A[mine] = t.astype(BF16)
            return 0

        lax.fori_loop(0, 16, body, 0)
        for d in (2, 1, 3):
            at = (me[b] + d) % 4
            go(p, {c: me[c], b: at}, {b: d}, r2.at[p, d - 1], 2 + d, St2.at[p, at], s2.at[p, d - 1])
    for p, (a, b, c) in enumerate(ORDERS):
        for d in (1, 2, 3):
            landed(p, r2.at[p, d - 1], 2 + d, s2.at[p, d - 1])
        stats = [St2[p, me[b]]] + [s2[p, d] for d in range(3)]
        top, tot, ws = merge([(s[0:4], s[4:8]) for s in stats])
        for i in range(4):
            idx = {c: me[c], b: me[b], a: i}
            mine = (idx["y"], k, idx["x"], idx["z"]) + QPARTS[p]
            t = A[mine].astype(F32) * ws[0][i : i + 1]
            for d in range(3):
                t += r2[p, d, i].astype(F32) * ws[d + 1][i : i + 1]
            A[mine] = t.astype(BF16)
            St3[p, i, 0:1] = top[i : i + 1]
            St3[p, i, 1:2] = tot[i : i + 1]
        for d in (2, 1, 3):
            at = (me[a] + d) % 4
            go(p, {c: me[c], b: me[b], a: at}, {a: d}, r3.at[p, d - 1], 5 + d, St3.at[p, at], s3.at[p, d - 1])
    for p, (a, b, c) in enumerate(ORDERS):
        for d in (1, 2, 3):
            landed(p, r3.at[p, d - 1], 5 + d, s3.at[p, d - 1])
        stats = [St3[p, me[a]]] + [s3[p, d] for d in range(3)]
        top, tot, ws = merge([(s[0:1], s[1:2]) for s in stats])
        t = A[(me["y"], k, me["x"], me["z"]) + QPARTS[p]].astype(F32) * ws[0]
        for d in range(3):
            t += r3[p, d].astype(F32) * ws[d + 1]
        t = t / tot
        both = jnp.concatenate([t, pltpu.roll(t, 64, 1)], axis=0)
        U[64 * p : 64 * p + 64, :] = both.T[:64]
    for c in range(16):
        rows = []
        for hh in range(3):
            h = 3 * c + hh
            rows.append(U[pl.ds((h // 16) * 64 + h % 16, 4, stride=16), :])
        G[c] = jnp.concatenate(rows + [jnp.zeros((4, 128), F32)], axis=0).astype(BF16)
    col = me["x"] * 4 + me["z"]
    steps = [(dx, dz) for dz in (2, 1, 3, 0) for dx in (2, 1, 3, 0) if dx or dz]

    def peer(dx, dz):
        return ((me["x"] + dx) % 4) * 4 + (me["z"] + dz) % 4

    for dx, dz in steps:
        c = remote(G.at[peer(dx, dz)], H.at[col], as_.at[dx * 4 + dz], ar.at[dx * 4 + dz], device(me, x=dx, z=dz))
        c.start()
        started.append(c)
    H[col] = G[col]
    for d in (1, 2, 3):
        there = hrec.at[(me["z"] - d) % 4]
        remote(there, there, hs.at[d - 1], hr.at[d - 1], device(me, k=1)).wait_recv()
    for z in range(4):
        f = hrec[z].astype(F32)
        hid[4 * z : 4 * z + 4, :] = jnp.concatenate([f[4 * q : 4 * q + 4] for q in range(4)], axis=1)
    wo_load.wait()
    for dx, dz in steps:
        there = H.at[peer(-dx, -dz)]
        remote(there, there, as_.at[dx * 4 + dz], ar.at[dx * 4 + dz], device(me, k=1)).wait_recv()
    heads = []
    hf = [H[c].astype(F32) for c in range(16)]
    for hh in range(3):
        heads.append(jnp.concatenate([hf[c][4 * hh : 4 * hh + 4] for c in range(16)], axis=0).astype(BF16))
    lhs = jnp.concatenate(heads, axis=1)
    for dz in (2, 1, 3, 0):
        zz = (me["z"] + dz) % 4
        res = jnp.dot(lhs, WO[:, pl.ds(pl.multiple_of(zz * 1536, 1536), 1536)], preferred_element_type=F32).astype(BF16)
        for x in range(4):
            O[x, zz] = res[16 * x : 16 * x + 16]
        for dx in (2, 1, 3, 0):
            if dx or dz:
                c = remote(O.at[(me["x"] + dx) % 4, zz], Rv.at[col], ps.at[dx * 4 + dz], pr.at[dx * 4 + dz], device(me, x=dx, z=dz))
                c.start()
                started.append(c)
    Rv[col] = O[me["x"], me["z"]]
    for dx, dz in steps:
        there = Rv.at[peer(-dx, -dz)]
        remote(there, there, ps.at[dx * 4 + dz], pr.at[dx * 4 + dz], device(me, k=1)).wait_recv()
    total = Rv[0].astype(F32)
    for c in range(1, 16):
        total += Rv[c].astype(F32)
    res = (hid[...] + total).astype(BF16)
    rb_o[...] = res
    f = res.astype(F32)
    xb_o[:, 0:1536] = (f * gain[me["z"]]).astype(BF16)
    squares = jnp.sum(f * f, axis=1, keepdims=True)
    high = squares.astype(BF16).astype(F32)
    low = squares - high
    ln = lax.broadcasted_iota(jnp.int32, (16, 128), 1)
    tile = jnp.where(ln == 0, high, jnp.where(ln == 1, low, gtile[...].astype(F32)))
    xb_o[:, 1536:1664] = tile.astype(BF16)
    for c in started:
        c.wait_send()


def attend_call(req, seen, prev, last, qb, nk, nvt, hin, gain, gtile, kv, wo, cid):
    V = pltpu.VMEM
    SM = pl.BlockSpec(memory_space=pltpu.SMEM)
    return pl.pallas_call(
        attend_kernel,
        out_shape=(jax.ShapeDtypeStruct((16, 1664), BF16), jax.ShapeDtypeStruct((16, 1536), BF16)),
        in_specs=[SM] * 4 + [VM] * 6 + [ANY, ANY],
        out_specs=(VM, VM),
        scratch_shapes=[
            V((4, 2, 4, 4, 192, 128), BF16), V((4, 2, 4, 4, 192, 128), BF16), V((32, 16, 2048), BF16), V((32, 128, 128), BF16),
            V((384, 6144), BF16), V((36, 128, 192), F32), V((36, 1, 192), F32), V((36, 1, 192), F32),
            V((36, 3, 64, 128), BF16), V((36, 3, 1, 128), F32), V((36, 3, 1, 128), F32),
            V((3, 2, 4, 2, 16, 128), F32), V((3, 4, 2, 16, 128), F32), V((4, 4, 4, 192, 128), BF16),
            V((3, 3, 4, 4, 64, 128), BF16), V((3, 3, 4, 64, 128), BF16), V((3, 3, 64, 128), BF16),
            V((3, 3, 2, 16, 128), F32), V((3, 4, 8, 128), F32), V((3, 3, 8, 128), F32), V((3, 4, 8, 128), F32), V((3, 3, 8, 128), F32),
            V((4, 16, 128), F32), V((192, 128), F32), V((16, 16, 128), BF16), V((16, 16, 128), BF16),
            V((4, 4, 16, 1536), BF16), V((16, 16, 1536), BF16), V((16, 1536), F32), V((4, 16, 384), BF16),
            DMA((2,)), DMA((3, 18)), DMA((3, 18)), DMA((3, 7)), DMA((3, 7)), DMA((3, 9)), DMA((3, 9)), DMA((3, 9)), DMA((3, 9)),
            DMA((3,)), DMA((3,)), DMA((3,)), DMA((3,)), DMA((3,)), DMA((3,)), DMA((16,)), DMA((16,)), DMA((16,)), DMA((16,)),
        ],
        compiler_params=pltpu.CompilerParams(collective_id=cid, has_side_effects=True, vmem_limit_bytes=60 * 2**20),
    )(req, seen, prev, last, qb, nk, nvt, hin, gain, gtile, kv, wo)


def on_device(hidden_in, queries, new_kv, kv_pool, block_table, cached_len, w_out, norm_gain, expert_ids, expert_gates,
              w_gate, w_up, w_down):
    rank = lax.axis_index(("row", "col"))
    z = lax.axis_index("col") % 4
    requests, blocks = block_table.shape
    ids = jnp.arange(requests, dtype=jnp.int32)[:, None]
    places = jnp.arange(blocks, dtype=jnp.int32)[None, :]
    visible = jnp.clip(cached_len[:, None] - 16 * places, 0, 16)
    code = ids * 32 + visible
    slots = rank * 32 + jnp.arange(32, dtype=jnp.int32)
    found = jnp.max(jnp.where(block_table[None] == slots[:, None, None], code[None], -1), axis=(1, 2))
    own = rank * 2 + jnp.arange(2, dtype=jnp.int32)
    owner = jnp.concatenate([jnp.where(found >= 0, found // 32, -1), own])
    seen = jnp.concatenate([jnp.where(found >= 0, found % 32, 0), jnp.zeros((2,), jnp.int32)])
    js = jnp.arange(34, dtype=jnp.int32)
    earlier = (owner[:, None] == owner[None, :]) & (js[None, :] < js[:, None]) & (owner[:, None] >= 0)
    prev = jnp.max(jnp.where(earlier, js[None, :], -1), axis=1)
    prev = jnp.where(prev < 0, EMPTY, prev)
    rs = jnp.arange(256, dtype=jnp.int32)
    last = jnp.max(jnp.where(owner[None, :] == rs[:, None], js[None, :], -1), axis=1)
    last = jnp.where(last < 0, EMPTY + rs % 2, last)
    pair = jnp.arange(2, dtype=jnp.int32)
    req = jnp.concatenate([jnp.maximum(owner, 0), pair])
    prev = jnp.concatenate([prev, jnp.full((2,), EMPTY, jnp.int32)])
    qb = jnp.transpose(queries.reshape(2, 2, 3, 16, 128), (2, 0, 1, 3, 4)).reshape(192, 128)
    fresh = new_kv.reshape(2, 2, 2, 8, 128)
    nk = jnp.transpose(fresh[:, :, 0], (0, 2, 1, 3)).reshape(2, 16, 128)
    nvt = jnp.transpose(fresh[:, :, 1], (0, 3, 2, 1)).reshape(2, 128, 16)
    hin = jnp.transpose(hidden_in.reshape(4, 4, 4, 384), (1, 2, 0, 3)).reshape(4, 16, 384)
    gain = norm_gain.astype(F32).reshape(4, 1, 1536)
    picks, gates = expert_ids.reshape(4, 2), expert_gates.reshape(4, 2)
    dense = jnp.sum(jnp.where(picks[:, :, None] == jnp.arange(8)[None, None], gates[:, :, None], 0.0), axis=1)
    high = dense.astype(BF16).astype(F32)
    rows = jnp.concatenate([jnp.zeros((4, 8), F32), high, dense - high, jnp.zeros((4, 104), F32)], axis=1)
    gtile = jnp.where((jnp.arange(16) // 4 == z)[:, None], jnp.tile(rows, (4, 1)), 0.0).astype(BF16)
    xb, rb = attend_call(req, seen, prev, last, qb, nk, nvt, hin, gain, gtile, kv_pool, w_out, 0)
    o = experts_call(xb, rb, w_gate[0], w_up[0], w_down[0], 1)
    return jnp.transpose(o.reshape(4, 4, 4, 384), (2, 0, 1, 3)).reshape(2, 2, 6144)


def solution(mesh):
    both = ("row", "col")
    return jax.shard_map(
        on_device,
        mesh=mesh,
        in_specs=(P(both, None, None), P(both, None, None), P(both, None, None), P(both, None, None), P(), P(), P("col", None),
                  P(), P(both, None, None), P(both, None, None), P("row", None, "col"), P("row", None, "col"), P("row", "col", None)),
        out_specs=P(both, None, None),
        check_vma=False,
    )
```

```python
import jax, functools
import jax.numpy as jnp
from jax import lax
from jax.experimental import pallas as pl
from jax.experimental.pallas import tpu as pltpu
from jax.sharding import PartitionSpec as P

MESH = pl.DeviceIdType.MESH
ORDERS = (("x", "y", "z"), ("y", "z", "x"), ("z", "x", "y"))
F32, BF16 = jnp.float32, jnp.bfloat16


def where_am_i():
    r, c = lax.axis_index("row"), lax.axis_index("col")
    return {"y": r // 2, "k": r % 2, "x": c // 4, "z": c % 4}


def device(me, **moved):
    at = dict(me)
    for name, step in moved.items():
        at[name] = (me[name] + step) % (2 if name == "k" else 4)
    return (at["y"] * 2 + at["k"], at["x"] * 4 + at["z"])


def pick(sel, name):
    return sel.get(name, slice(None))


def block_of(ref, k, sel, part):
    return ref.at[(pick(sel, "y"), k, pick(sel, "x"), pick(sel, "z")) + part]


def remote(src, dst, send, recv, where):
    return pltpu.make_async_remote_copy(
        src_ref=src, dst_ref=dst, send_sem=send, recv_sem=recv, device_id=where, device_id_type=MESH
    )


def greet(me, plane=False):
    bar = pltpu.get_barrier_semaphore()
    count = 0
    for name in ("x", "y", "z"):
        for d in (1, 2, 3):
            pl.semaphore_signal(bar, inc=1, device_id=device(me, **{name: d}), device_id_type=MESH)
            count += 1
    pl.semaphore_signal(bar, inc=1, device_id=device(me, k=1), device_id_type=MESH)
    count += 1
    if plane:
        for dx in (1, 2, 3):
            for dz in (1, 2, 3):
                pl.semaphore_signal(bar, inc=1, device_id=device(me, x=dx, z=dz), device_id_type=MESH)
                count += 1
    pl.semaphore_wait(bar, count)


def shift(me, **moved):
    return {n: (me[n] - s) % 4 for n, s in moved.items()}


HALF = (slice(0, 2), slice(2, 4))


def gather_blocks(buf, me, parts, send, recv, cs, cr, hooks=(), on_line=None):
    k = me["k"]
    started = []

    def go(p, sel, moved, i):
        there = block_of(buf, k, sel, parts[p])
        copy = remote(there, there, send.at[p, i], recv.at[p, i], device(me, **moved))
        copy.start()
        started.append(copy)

    def landed(p, sel, i):
        here = block_of(buf, k, sel, parts[p])
        remote(here, here, send.at[p, i], recv.at[p, i], device(me, k=1)).wait_recv()

    def across(p, sel, i, kk=k):
        there = block_of(buf, kk, sel, parts[p])
        return remote(there, there, cs.at[p, i], cr.at[p, i], device(me, k=1))

    def cross(p, sel, i):
        copy = across(p, sel, i)
        copy.start()
        started.append(copy)

    for p, (a, b, c) in enumerate(ORDERS):
        for d in (2, 1, 3):
            go(p, {n: me[n] for n in "xyz"}, {a: d}, d - 1)
    if hooks:
        hooks[0]()
    for p, (a, b, c) in enumerate(ORDERS):
        for d in (1, 3, 2):
            landed(p, {a: (me[a] - d) % 4, b: me[b], c: me[c]}, d - 1)
        for d in (2, 1, 3):
            go(p, {b: me[b], c: me[c]}, {b: d}, 3 + d - 1)
    if hooks:
        hooks[1]()
    for p, (a, b, c) in enumerate(ORDERS):
        for d in (1, 3, 2):
            landed(p, {b: (me[b] - d) % 4, c: me[c]}, 3 + d - 1)
        go(p, {b: HALF[0], c: me[c]}, {c: 1}, 6)
        go(p, {b: HALF[1], c: me[c]}, {c: -1}, 9)
        go(p, {b: HALF[1], c: me[c]}, {c: 1}, 7)
        go(p, {b: HALF[0], c: me[c]}, {c: -1}, 8)
        cross(p, {c: me[c]}, 0)
    if hooks:
        hooks[2]()

    def both_cores(i, d):
        for p, (a, b, c) in enumerate(ORDERS):
            across(p, {c: (me[c] + d) % 4}, i, 1 - k).wait_recv()
        if on_line:
            on_line(d)

    for p, (a, b, c) in enumerate(ORDERS):
        landed(p, {b: HALF[0], c: (me[c] - 1) % 4}, 6)
        go(p, {b: HALF[0], c: (me[c] - 1) % 4}, {c: 1}, 10)
        landed(p, {b: HALF[1], c: (me[c] + 1) % 4}, 9)
        go(p, {b: HALF[1], c: (me[c] + 1) % 4}, {c: -1}, 11)
    both_cores(0, 0)
    for p, (a, b, c) in enumerate(ORDERS):
        landed(p, {b: HALF[1], c: (me[c] - 1) % 4}, 7)
        cross(p, {c: (me[c] - 1) % 4}, 1)
        landed(p, {b: HALF[0], c: (me[c] + 1) % 4}, 8)
        cross(p, {c: (me[c] + 1) % 4}, 2)
    both_cores(1, 3)
    both_cores(2, 1)
    for p, (a, b, c) in enumerate(ORDERS):
        landed(p, {b: HALF[0], c: (me[c] + 2) % 4}, 10)
        landed(p, {b: HALF[1], c: (me[c] + 2) % 4}, 11)
        cross(p, {c: (me[c] + 2) % 4}, 3)
    both_cores(3, 2)
    for copy in started:
        copy.wait_send()


def send_core(buf, me, parts, core, cs, cr, p):
    copy = remote(
        buf.at[(slice(None), 1 - me["k"], slice(None), slice(None)) + parts[p]],
        core.at[(slice(None), slice(None), slice(None)) + parts[p]],
        cs.at[p], cr.at[p], device(me, k=1),
    )
    copy.start()
    return copy


def scatter_blocks(buf, me, parts, fwd, line, r2, r3, send, recv, started, ready):
    k = me["k"]

    def go(p, sel, moved, dst, i):
        copy = remote(block_of(buf, k, sel, parts[p]), dst, send.at[p, i], recv.at[p, i], device(me, **moved))
        copy.start()
        started.append(copy)

    def landed(p, dst, i):
        remote(dst, dst, send.at[p, i], recv.at[p, i], device(me, k=1)).wait_recv()

    def rest_of(c):
        return [n for n in ("y", "x", "z") if n != c]

    def sub(ref, p, j, b, c, half):
        return ref.at[(p, j) + tuple(HALF[half] if n == b else slice(None) for n in rest_of(c))]

    def add(p, b, c, at, half, terms):
        rest = rest_of(c)

        def body(n, _):
            i_b, i_a = 2 * half + n // 4, n % 4
            idx = {c: at, **{m: (i_b if m == b else i_a) for m in rest}}
            mine = (idx["y"], k, idx["x"], idx["z"]) + parts[p]
            total = buf[mine].astype(F32)
            for t in terms:
                total += t(idx, rest, n).astype(F32)
            buf[mine] = total.astype(BF16)
            return 0

        lax.fori_loop(0, 8, body, 0, unroll=4)

    for p, (a, b, c) in enumerate(ORDERS):
        ready(p)
        far, right, left = (me[c] + 2) % 4, (me[c] + 1) % 4, (me[c] - 1) % 4
        go(p, {c: far, b: HALF[0]}, {c: 1}, fwd_dst(fwd, p, 0, a, b, c), 0)
        go(p, {c: far, b: HALF[1]}, {c: -1}, fwd_dst(fwd, p, 1, a, b, c), 1)
        go(p, {c: right, b: HALF[1]}, {c: 1}, sub(line, p, 0, b, c, 1), 2)
        go(p, {c: left, b: HALF[0]}, {c: -1}, sub(line, p, 1, b, c, 0), 3)
    for p, (a, b, c) in enumerate(ORDERS):
        right, left = (me[c] + 1) % 4, (me[c] - 1) % 4
        landed(p, fwd_dst(fwd, p, 0, a, b, c), 0)
        add(p, b, c, right, 0, [fwd_at(fwd, p, 0, a, b, c)])
        go(p, {c: right, b: HALF[0]}, {c: 1}, sub(line, p, 0, b, c, 0), 4)
        landed(p, fwd_dst(fwd, p, 1, a, b, c), 1)
        add(p, b, c, left, 1, [fwd_at(fwd, p, 1, a, b, c)])
        go(p, {c: left, b: HALF[1]}, {c: -1}, sub(line, p, 1, b, c, 1), 5)
    for p, (a, b, c) in enumerate(ORDERS):
        for i, (j, h) in ((2, (0, 1)), (3, (1, 0)), (4, (0, 0)), (5, (1, 1))):
            landed(p, sub(line, p, j, b, c, h), i)
        def lt(j, p=p):
            return lambda idx, rest, n: line[p, j, idx[rest[0]], idx[rest[1]]]
        for h in range(2):
            add(p, b, c, me[c], h, [lt(0), lt(1)])
        for d in (2, 1, 3):
            go(p, {c: me[c], b: (me[b] + d) % 4}, {b: d}, r2.at[p, d - 1], 5 + d)
    for p, (a, b, c) in enumerate(ORDERS):
        for d in (1, 2, 3):
            landed(p, r2.at[p, d - 1], 5 + d)
        for i in range(4):
            idx = {c: me[c], b: me[b], a: i}
            mine = (idx["y"], k, idx["x"], idx["z"]) + parts[p]
            total = buf[mine].astype(F32)
            for d in range(3):
                total += r2[p, d, i].astype(F32)
            buf[mine] = total.astype(BF16)
        for d in (2, 1, 3):
            go(p, {c: me[c], b: me[b], a: (me[a] + d) % 4}, {a: d}, r3.at[p, d - 1], 8 + d)
    sums = []
    for p, (a, b, c) in enumerate(ORDERS):
        for d in (1, 2, 3):
            landed(p, r3.at[p, d - 1], 8 + d)
        total = buf[(me["y"], k, me["x"], me["z"]) + parts[p]].astype(F32)
        for d in range(3):
            total += r3[p, d].astype(F32)
        sums.append(total)
    for copy in started:
        copy.wait_send()
    return sums


def half_first(a, b, c):
    rest = [n for n in ("y", "x", "z") if n != c]
    return rest[0] == b


def fwd_dst(fwd, p, j, a, b, c):
    return fwd[half_first(a, b, c)].at[p, j]


def fwd_at(fwd, p, j, a, b, c):
    if half_first(a, b, c):
        return lambda idx, rest, n: fwd[True][p, j, n // 4, n % 4]
    return lambda idx, rest, n: fwd[False][p, j, n % 4, n // 4]


QPARTS = [(slice(64 * p, 64 * p + 64), slice(None)) for p in range(3)]
EMPTY = 34


def layer_kernel(table, clen, ids, gates, queries, new_kv, hidden, gain, kv_h, wo_h, wg_h, wu_h, wd_h, o_ref,
                 X, A, KV, VT, WO, WG, WU, WD, accs, ms, ls, Z, Zm, Zl, St, Cst, core, fa, fb, line, r2, r3, sf, sl, St2, s2, St3, s3, Wt,
                 U, NK, NV, GF, CC, info_v, info, G, H, O, Rv, hid, hin, hrec, acc, act, scal, resid, fout, fin,
                 lsem, gs, gr, gcs, gcr, ss_, sr, ts, tr, scs, scr, tcs, tcr, hs, hr, as_, ar, ps, pr,
                 gs2, gr2, gcs2, gcr2, ss2, sr2, scs2, scr2, fs, fr):
    me = where_am_i()
    k = me["k"]
    rank = me["y"] * 32 + k * 16 + me["x"] * 4 + me["z"]
    kv_load = pltpu.make_async_copy(kv_h, KV, lsem.at[0])
    wo_load = pltpu.make_async_copy(wo_h, WO, lsem.at[1])
    loads = [pltpu.make_async_copy(h.at[0], v, lsem.at[2 + i]) for i, (h, v) in enumerate(((wg_h, WG), (wu_h, WU), (wd_h, WD)))]
    info_load = pltpu.make_async_copy(info_v, info, lsem.at[5])
    kv_load.start()
    wo_load.start()
    for c in loads:
        c.start()
    for i in range(2):
        q = queries[i].astype(F32)
        for h in range(48):
            U[pl.ds((h // 16) * 64 + i * 32 + h % 16, 2, stride=16), :] = q[:, 128 * h : 128 * h + 128]
    X[me["y"], k, me["x"], me["z"], 0:192, :] = U[...].astype(BF16)
    greet(me, plane=True)
    started = []

    def find_blocks():
        code = lax.broadcasted_iota(jnp.int32, (64, 256), 1) * 64 + lax.broadcasted_iota(jnp.int32, (64, 256), 0)

        def search(j, _):
            CC[pl.ds(j, 1), :] = jnp.max(jnp.where(table[...] == rank * 32 + j, code, -1), axis=0, keepdims=True)
            return 0

        lax.fori_loop(0, 32, search, 0, unroll=4)
        CC[32:40, :] = jnp.full((8, 256), -1, jnp.int32)
        found = jnp.max(CC[...], axis=1, keepdims=True)
        r = lax.broadcasted_iota(jnp.int32, (40, 128), 0)
        c = lax.broadcasted_iota(jnp.int32, (40, 128), 1)
        found = jnp.broadcast_to(found, (40, 128))
        found = jnp.where((r == 32) | (r == 33), (rank * 2 + r - 32) * 64, found)
        owner = jnp.where(found >= 0, found // 64, -1)
        as_row = lambda v: jnp.max(jnp.where(r == c, v, -1), axis=0, keepdims=True)
        owner_row, place_row = as_row(owner), as_row(jnp.where(found >= 0, found % 64, 0))
        before = jnp.max(jnp.where((owner == owner_row) & (r < c) & (owner >= 0), r, -1), axis=0, keepdims=True)
        info_v[1:2, 0:128] = jnp.where(before < 0, EMPTY, before)
        cr = c[0:1]
        info_v[2:3, 0:128] = jnp.where(cr < 34, jnp.maximum(owner_row, 0), jnp.where(cr == 35, 1, 0))
        info_v[3:4, 0:128] = jnp.maximum(place_row, 0)
        r2_ = lax.broadcasted_iota(jnp.int32, (40, 256), 0)
        c2_ = lax.broadcasted_iota(jnp.int32, (40, 256), 1)
        owner2 = jnp.concatenate([owner, owner], axis=1)
        last_ = jnp.max(jnp.where(owner2 == c2_, r2_, -1), axis=0, keepdims=True)
        info_v[0:1, :] = jnp.where(last_ < 0, EMPTY + c2_[0:1] % 2, last_)
        info_load.start()

    def small_things():
        for i in range(2):
            v = new_kv[i].astype(F32)
            for g in range(8):
                NK[i, 2 * g : 2 * g + 2, :] = v[:, 128 * g : 128 * g + 128]
                NV[i, 2 * g : 2 * g + 2, :] = v[:, 1024 + 128 * g : 1152 + 128 * g]
        GF[...] = gain[...].astype(F32)
        f = jnp.concatenate([hidden[0].astype(F32), hidden[1].astype(F32)], axis=0)
        for z in range(4):
            hin[z] = jnp.concatenate([f[:, 1536 * z + 384 * q : 1536 * z + 384 * q + 384] for q in range(4)], axis=0).astype(BF16)
        for d in (1, 2, 3):
            c = remote(hin.at[(me["z"] + d) % 4], hrec.at[me["z"]], hs.at[d - 1], hr.at[d - 1], device(me, z=d))
            c.start()
            started.append(c)
        hrec[me["z"]] = hin[me["z"]]

    def turn_values():
        kv_load.wait()

        def turn(j, _):
            v = jnp.concatenate([KV[j, :, 1024 + 128 * g : 1152 + 128 * g] for g in range(8)], axis=0)
            VT[j] = v.astype(F32).T.astype(BF16)
            return 0

        lax.fori_loop(0, 32, turn, 0, unroll=4)
        fresh_slots()

    lane = lax.broadcasted_iota(jnp.int32, (128, 192), 1)
    rowi = lax.broadcasted_iota(jnp.int32, (128, 192), 0)
    head_kv = ((lane // 64) * 16 + lane % 16) // 6
    lane_i = (lane // 32) % 2
    lane_s = (lane // 16) % 2
    same = jnp.where(head_kv == rowi // 16, rowi % 16, 99)

    def fresh_slots():
        own = X[me["y"], k, me["x"], me["z"], 0:192, :]
        for i in range(2):
            st = lax.dot_general(NK[i].astype(BF16), own, (((1,), (1,)), ((), ())), preferred_element_type=F32) * (128 ** -0.5)
            r = rowi[:16]
            ok = (head_kv[:16] == r // 2) & (r % 2 <= lane_s[:16]) & (lane_i[:16] == i)
            st = jnp.where(ok, st, -1e30)
            m = jnp.max(st, axis=0, keepdims=True)
            w = jnp.exp(st - m)
            accs[32 + i] = jnp.dot(NV[i].T.astype(BF16), w.astype(BF16), preferred_element_type=F32)
            ms[32 + i] = m
            ls[32 + i] = jnp.sum(w, axis=0, keepdims=True)
            accs[EMPTY + i] = jnp.zeros((128, 192), F32)
            ms[EMPTY + i] = jnp.full((1, 192), -1e30, F32)
            ls[EMPTY + i] = jnp.zeros((1, 192), F32)

    gather_blocks(X, me, QPARTS, gs, gr, gcs, gcr, (find_blocks, small_things, turn_values))
    info_load.wait()

    def slot(j, _):
        rq = info[2, j]
        seen = jnp.clip(clen[rq] - 16 * info[3, j], 0, 16)
        q = X[rq // 64, (rq // 32) % 2, (rq // 8) % 4, (rq // 2) % 4, 0:192, :]
        ks = jnp.concatenate([KV[j, :, 128 * g : 128 * g + 128] for g in range(8)], axis=0)
        st = lax.dot_general(ks, q, (((1,), (1,)), ((), ())), preferred_element_type=F32) * (128 ** -0.5)
        st = jnp.where((same < seen) & (lane_i == rq % 2), st, -1e30)
        m = jnp.max(st, axis=0, keepdims=True)
        w = jnp.exp(st - m)
        accs[j] = jnp.dot(VT[j], w.astype(BF16), preferred_element_type=F32)
        ms[j] = m
        ls[j] = jnp.sum(w, axis=0, keepdims=True)
        return 0

    lax.fori_loop(0, 32, slot, 0, unroll=4)
    def chain(j, _):
        pj = info[1, j]
        i = info[2, j] % 2
        m0, m1 = ms[j], ms[pj]
        m = jnp.maximum(m0, m1)
        w0, w1 = jnp.exp(m0 - m), jnp.exp(m1 - m)
        acc = accs[j] * w0 + accs[pj] * w1
        l = ls[j] * w0 + ls[pj] * w1
        accs[j] = acc
        ms[j] = m
        ls[j] = l
        mine = lane_i == i
        acc = jnp.where(mine, acc, 0.0)
        m = jnp.where(mine[:1], m, 0.0)
        l = jnp.where(mine[:1], l, 0.0)
        for p in range(3):
            s = slice(64 * p, 64 * p + 64)
            Z[j, p] = jnp.concatenate([acc[:64, s], acc[64:, s]], axis=1).astype(BF16)
            Zm[j, p] = jnp.concatenate([m[:, s], m[:, s]], axis=1)
            Zl[j, p] = jnp.concatenate([l[:, s], l[:, s]], axis=1)
        return 0

    lax.fori_loop(0, 36, chain, 0, unroll=2)

    def spread(kk, ps_):
        def body(n, _):
            y, x, z = n // 16, (n // 4) % 4, n % 4
            to = y * 32 + kk * 16 + x * 4 + z
            s0, s1_ = info[0, 2 * to], info[0, 2 * to + 1]
            at = {"y": y, "x": x, "z": z}
            for p in ps_:
                a, b, c = ORDERS[p]
                A[y, kk, x, z, 64 * p : 64 * p + 64, :] = Z[s0, p] + Z[s1_, p]
                row = pl.ds((at[b] % 2) * 4 + at[a], 1)
                St[p, kk, at[c], at[b] // 2, 0, row, :] = Zm[s0, p] + Zm[s1_, p]
                St[p, kk, at[c], at[b] // 2, 1, row, :] = Zl[s0, p] + Zl[s1_, p]
            return 0

        lax.fori_loop(0, 64, body, 0, unroll=4)

    cores = []
    for p in range(3):
        spread(1 - k, (p,))
        c0 = send_core(A, me, QPARTS, core, scs, scr, p)
        c1 = remote(St.at[p, 1 - k], Cst.at[p], tcs.at[p], tcr.at[p], device(me, k=1))
        c1.start()
        cores.append((c0, c1))
        started.extend((c0, c1))
    spread(k, (0, 1, 2))

    def go(p, sel, moved, dst, i, stat, sdst):
        c0 = remote(block_of(A, k, sel, QPARTS[p]), dst, ss_.at[p, i], sr.at[p, i], device(me, **moved))
        c1 = remote(stat, sdst, ts.at[p, i], tr.at[p, i], device(me, **moved))
        c0.start()
        c1.start()
        started.extend((c0, c1))

    def landed(p, dst, i, sdst):
        remote(dst, dst, ss_.at[p, i], sr.at[p, i], device(me, k=1)).wait_recv()
        remote(sdst, sdst, ts.at[p, i], tr.at[p, i], device(me, k=1)).wait_recv()

    def merge(stats):
        top = functools.reduce(jnp.maximum, [m for m, _ in stats])
        ws = [jnp.exp(m - top) for m, _ in stats]
        return top, sum(w * l for w, (_, l) in zip(ws, stats)), ws

    def others(c):
        return [n for n in ("y", "x", "z") if n != c]

    fwd = {True: fa, False: fb}

    def half_line(p, j, b, c, h):
        return line.at[(p, j) + tuple(HALF[h] if n == b else slice(None) for n in others(c))]

    def blend(p, at, h, sources):
        a, b, c = ORDERS[p]
        here = St[p, k, at, h]
        stats = [(here[0], here[1])] + [(s[0], s[1]) for _, s in sources]
        top, tot, ws = merge(stats)
        St[p, k, at, h, 0] = top
        St[p, k, at, h, 1] = tot
        for i, w in enumerate(ws):
            Wt[i] = w

        def body(n, _):
            idx = {c: at, b: 2 * h + n // 4, a: n % 4}
            row = pl.ds(n, 1)
            mine = (idx["y"], k, idx["x"], idx["z"]) + QPARTS[p]
            t = A[mine].astype(F32) * Wt[0, row, :]
            for i, (block, _) in enumerate(sources):
                t += block(idx, n).astype(F32) * Wt[i + 1, row, :]
            A[mine] = t.astype(BF16)
            return 0

        lax.fori_loop(0, 8, body, 0, unroll=4)

    def from_core(p, at, h):
        return (lambda idx, n: core[(idx["y"], idx["x"], idx["z"]) + QPARTS[p]]), Cst[p, at, h]

    def from_fwd(p, j):
        a, b, c = ORDERS[p]
        get = fwd_at(fwd, p, j, a, b, c)
        return (lambda idx, n: get(idx, None, n)), sf[p, j]

    def from_line(p, j, h):
        rest = others(ORDERS[p][2])
        return (lambda idx, n: line[p, j, idx[rest[0]], idx[rest[1]]]), sl[p, j, h]

    for p, (a, b, c) in enumerate(ORDERS):
        for copy in cores[p]:
            copy.wait_recv()
        far, right, left = (me[c] + 2) % 4, (me[c] + 1) % 4, (me[c] - 1) % 4
        blend(p, far, 0, [from_core(p, far, 0)])
        go(p, {c: far, b: HALF[0]}, {c: 1}, fwd_dst(fwd, p, 0, a, b, c), 0, St.at[p, k, far, 0], sf.at[p, 0])
        blend(p, far, 1, [from_core(p, far, 1)])
        go(p, {c: far, b: HALF[1]}, {c: -1}, fwd_dst(fwd, p, 1, a, b, c), 1, St.at[p, k, far, 1], sf.at[p, 1])
        blend(p, right, 1, [from_core(p, right, 1)])
        go(p, {c: right, b: HALF[1]}, {c: 1}, half_line(p, 0, b, c, 1), 2, St.at[p, k, right, 1], sl.at[p, 0, 1])
        blend(p, left, 0, [from_core(p, left, 0)])
        go(p, {c: left, b: HALF[0]}, {c: -1}, half_line(p, 1, b, c, 0), 3, St.at[p, k, left, 0], sl.at[p, 1, 0])
    for p, (a, b, c) in enumerate(ORDERS):
        right, left = (me[c] + 1) % 4, (me[c] - 1) % 4
        landed(p, fwd_dst(fwd, p, 0, a, b, c), 0, sf.at[p, 0])
        blend(p, right, 0, [from_core(p, right, 0), from_fwd(p, 0)])
        go(p, {c: right, b: HALF[0]}, {c: 1}, half_line(p, 0, b, c, 0), 4, St.at[p, k, right, 0], sl.at[p, 0, 0])
        landed(p, fwd_dst(fwd, p, 1, a, b, c), 1, sf.at[p, 1])
        blend(p, left, 1, [from_core(p, left, 1), from_fwd(p, 1)])
        go(p, {c: left, b: HALF[1]}, {c: -1}, half_line(p, 1, b, c, 1), 5, St.at[p, k, left, 1], sl.at[p, 1, 1])
    for p, (a, b, c) in enumerate(ORDERS):
        for h in range(2):
            blend(p, me[c], h, [from_core(p, me[c], h)])
    for p, (a, b, c) in enumerate(ORDERS):
        for i, (j, h) in ((2, (0, 1)), (3, (1, 0)), (4, (0, 0)), (5, (1, 1))):
            landed(p, half_line(p, j, b, c, h), i, sl.at[p, j, h])
        for h in range(2):
            blend(p, me[c], h, [from_line(p, 0, h), from_line(p, 1, h)])
            for i in range(2):
                St2[p, 2 * h + i, 0:4] = St[p, k, me[c], h, 0, 4 * i : 4 * i + 4]
                St2[p, 2 * h + i, 4:8] = St[p, k, me[c], h, 1, 4 * i : 4 * i + 4]
        for d in (2, 1, 3):
            at = (me[b] + d) % 4
            go(p, {c: me[c], b: at}, {b: d}, r2.at[p, d - 1], 5 + d, St2.at[p, at], s2.at[p, d - 1])
    for p, (a, b, c) in enumerate(ORDERS):
        for d in (1, 2, 3):
            landed(p, r2.at[p, d - 1], 5 + d, s2.at[p, d - 1])
        stats = [St2[p, me[b]]] + [s2[p, d] for d in range(3)]
        top, tot, ws = merge([(s[0:4], s[4:8]) for s in stats])
        for i in range(4):
            idx = {c: me[c], b: me[b], a: i}
            mine = (idx["y"], k, idx["x"], idx["z"]) + QPARTS[p]
            t = A[mine].astype(F32) * ws[0][i : i + 1]
            for d in range(3):
                t += r2[p, d, i].astype(F32) * ws[d + 1][i : i + 1]
            A[mine] = t.astype(BF16)
            St3[p, i, 0:1] = top[i : i + 1]
            St3[p, i, 1:2] = tot[i : i + 1]
        for d in (2, 1, 3):
            at = (me[a] + d) % 4
            go(p, {c: me[c], b: me[b], a: at}, {a: d}, r3.at[p, d - 1], 8 + d, St3.at[p, at], s3.at[p, d - 1])
    for p, (a, b, c) in enumerate(ORDERS):
        for d in (1, 2, 3):
            landed(p, r3.at[p, d - 1], 8 + d, s3.at[p, d - 1])
        stats = [St3[p, me[a]]] + [s3[p, d] for d in range(3)]
        top, tot, ws = merge([(s[0:1], s[1:2]) for s in stats])
        t = A[(me["y"], k, me["x"], me["z"]) + QPARTS[p]].astype(F32) * ws[0]
        for d in range(3):
            t += r3[p, d].astype(F32) * ws[d + 1]
        t = t / tot
        both = jnp.concatenate([t, pltpu.roll(t, 64, 1)], axis=0)
        U[64 * p : 64 * p + 64, :] = both.T[:64]
    for c in range(16):
        rows = []
        for hh in range(3):
            h = 3 * c + hh
            rows.append(U[pl.ds((h // 16) * 64 + h % 16, 4, stride=16), :])
        G[c] = jnp.concatenate(rows + [jnp.zeros((4, 128), F32)], axis=0).astype(BF16)
    col = me["x"] * 4 + me["z"]
    steps = [(dx, dz) for dz in (2, 1, 3, 0) for dx in (2, 1, 3, 0) if dx or dz]

    def peer(dx, dz):
        return ((me["x"] + dx) % 4) * 4 + (me["z"] + dz) % 4

    for dx, dz in steps:
        c = remote(G.at[peer(dx, dz)], H.at[col], as_.at[dx * 4 + dz], ar.at[dx * 4 + dz], device(me, x=dx, z=dz))
        c.start()
        started.append(c)
    H[col] = G[col]
    for d in (1, 2, 3):
        there = hrec.at[(me["z"] - d) % 4]
        remote(there, there, hs.at[d - 1], hr.at[d - 1], device(me, k=1)).wait_recv()
    for z in range(4):
        f = hrec[z].astype(F32)
        hid[4 * z : 4 * z + 4, :] = jnp.concatenate([f[4 * q : 4 * q + 4] for q in range(4)], axis=1)
    wo_load.wait()
    for dx, dz in steps:
        there = H.at[peer(-dx, -dz)]
        remote(there, there, as_.at[dx * 4 + dz], ar.at[dx * 4 + dz], device(me, k=1)).wait_recv()
    heads = []
    hf = [H[c].astype(F32) for c in range(16)]
    for hh in range(3):
        heads.append(jnp.concatenate([hf[c][4 * hh : 4 * hh + 4] for c in range(16)], axis=0).astype(BF16))
    lhs = jnp.concatenate(heads, axis=1)
    for dz in (2, 1, 3, 0):
        zz = (me["z"] + dz) % 4
        res = jnp.dot(lhs, WO[:, pl.ds(pl.multiple_of(zz * 1536, 1536), 1536)], preferred_element_type=F32).astype(BF16)
        for x in range(4):
            O[x, zz] = res[16 * x : 16 * x + 16]
        for dx in (2, 1, 3, 0):
            if dx or dz:
                c = remote(O.at[(me["x"] + dx) % 4, zz], Rv.at[col], ps.at[dx * 4 + dz], pr.at[dx * 4 + dz], device(me, x=dx, z=dz))
                c.start()
                started.append(c)
    Rv[col] = O[me["x"], me["z"]]
    for dx, dz in steps:
        there = Rv.at[peer(-dx, -dz)]
        remote(there, there, ps.at[dx * 4 + dz], pr.at[dx * 4 + dz], device(me, k=1)).wait_recv()
    total = Rv[0].astype(F32)
    for c in range(1, 16):
        total += Rv[c].astype(F32)
    res = (hid[...] + total).astype(BF16)
    resid[...] = res
    f = res.astype(F32)
    xg = jnp.concatenate([f[:, 128 * c : 128 * c + 128] * GF[pl.ds(me["z"] * 12 + c, 1), :] for c in range(12)], axis=1).astype(BF16)
    squares = jnp.sum(f * f, axis=1, keepdims=True)
    high = squares.astype(BF16).astype(F32)
    low = squares - high
    ln = lax.broadcasted_iota(jnp.int32, (16, 128), 1)
    rw = lax.broadcasted_iota(jnp.int32, (16, 128), 0)
    gt = jnp.zeros((16, 128), F32)
    for t in range(4):
        for n in range(2):
            gt += jnp.where((rw == 4 * me["z"] + t) & (ln == 8 + ids[t // 2, t % 2, n]), gates[t // 2, t % 2, n], 0.0)
    gh = gt.astype(BF16).astype(F32)
    tile = gh + pltpu.roll(gt - gh, 8, 1)
    tile = jnp.where(ln == 0, high, jnp.where(ln == 1, low, tile)).astype(BF16)
    here = (me["y"], k, me["x"], me["z"])
    for c in range(12):
        X[here + (slice(16 * c, 16 * c + 16), slice(None))] = xg[:, 128 * c : 128 * c + 128]
    X[here + (slice(192, 208), slice(None))] = tile
    for c in started:
        c.wait_send()
    experts(me, X, WG, WU, WD, A, core, fwd, line, r2, r3, acc, act, scal, resid, fout, fin, loads,
            gs2, gr2, gcs2, gcr2, ss2, sr2, scs2, scr2, fs, fr, o_ref)


XPARTS = [(slice(0, 64), slice(None)), (slice(64, 128), slice(None)), (slice(128, 208), slice(None))]


def experts(me, X, WG, WU, WD, A, core, fwd, line, r2, r3, acc, act, scal, resid, fout, fin, loads,
            gs, gr, gcs, gcr, ss_, sr, scs, scr, fs, fr, o_ref):
    k = me["k"]
    expert = me["y"] * 2 + k
    acc[...] = jnp.zeros_like(acc)

    def add_product(at, rows, k0):
        x = jnp.concatenate([X[rows + (slice(16 * n, 16 * n + 16), slice(None))] for n in range(4 * k0[1], 4 * k0[1] + 4)], axis=-1)
        lead = x.shape[:-1]
        x = x.reshape(-1, 512)
        depth = pl.ds(pl.multiple_of(k0[0] * 1536 + 512 * k0[1], 512), 512)
        for n, W in enumerate((WG, WU)):
            for h in range(2):
                cols = slice(512 * n + 256 * h, 512 * n + 256 * h + 256)
                r = jnp.dot(x, W[depth, 256 * h : 256 * h + 256], preferred_element_type=F32)
                acc[at + (cols,)] += r.reshape(lead + (256,))

    def on_line(d):
        if d == 0:
            loads[0].wait()
            loads[1].wait()
        full = slice(None)
        z, x, y = (me["z"] + d) % 4, (me["x"] + d) % 4, (me["y"] + d) % 4
        add_product((full, full, full, full), (full, full, full, z), (z, 0))

        def body(zz, _):
            add_product((full, full, x, full), (full, full, x, zz), (zz, 1))
            add_product((y, full, full, full), (y, full, full, zz), (zz, 2))
            return 0

        lax.fori_loop(0, 4, body, 0)

    gather_blocks(X, me, XPARTS, gs, gr, gcs, gcr, (), on_line)
    loads[2].wait()
    extra = jnp.zeros((512, 128), F32)
    for z in range(4):
        extra += X[:, :, :, z, 192:208, :].reshape(512, 128).astype(F32)
    lane = lax.broadcasted_iota(jnp.int32, (512, 128), 1)
    squares = jnp.sum(jnp.where(lane < 3, extra, 0.0), axis=1, keepdims=True)
    weight = jnp.sum(jnp.where((lane == 8 + expert) | (lane == 16 + expert), extra, 0.0), axis=1, keepdims=True)
    scal[0] = jnp.broadcast_to(lax.rsqrt(squares * (1.0 / 6144.0) + 1e-5), (512, 128)).reshape(4, 2, 4, 16, 128)
    scal[1] = jnp.broadcast_to(weight, (512, 128)).reshape(4, 2, 4, 16, 128)
    started = []
    for kk in (1 - k, k):
        for n in range(4):
            at = (slice(None), kk, slice(None), slice(None))
            rs = scal[(0,) + at].reshape(256, 128)
            g = acc[at + (slice(128 * n, 128 * n + 128),)].reshape(256, 128) * rs
            u = acc[at + (slice(512 + 128 * n, 640 + 128 * n),)].reshape(256, 128) * rs
            v = g / (1.0 + jnp.exp(-g)) * u * scal[(1,) + at].reshape(256, 128)
            act[at + (slice(128 * n, 128 * n + 128),)] = v.astype(BF16).reshape(4, 4, 16, 128)

    def down(kk, p, with_core):
        def body(z, _):
            cols = pl.ds(pl.multiple_of(z * 1536 + 512 * p, 512), 512)
            r = jnp.dot(act[:, kk].reshape(256, 512), WD[:, cols], preferred_element_type=F32)
            for n in range(4):
                rows = slice(64 * p + 16 * n, 64 * p + 16 * n + 16)
                t = r[:, 128 * n : 128 * n + 128].reshape(4, 4, 16, 128)
                if with_core:
                    t += core[:, :, z, rows, :].astype(F32)
                A[:, kk, :, z, rows, :] = t.astype(BF16)
            return 0

        lax.fori_loop(0, 4, body, 0)

    for p in range(3):
        down(1 - k, p, False)
        started.append(send_core(A, me, QPARTS, core, scs, scr, p))

    def ready(p):
        started[p].wait_recv()
        down(k, p, True)

    sums = scatter_blocks(A, me, QPARTS, fwd, line, r2, r3, ss_, sr, started, ready)
    total = jnp.concatenate([s[16 * c : 16 * c + 16] for s in sums for c in range(4)], axis=1) + resid[...].astype(F32)
    for z in range(4):
        rows = total[4 * z : 4 * z + 4]
        fout[z] = jnp.concatenate([rows[:, 384 * q : 384 * q + 384] for q in range(4)], axis=0).astype(BF16)
    outs = []
    for d in (2, 1, 3):
        c = remote(fout.at[(me["z"] + d) % 4], fin.at[me["z"]], fs.at[d - 1], fr.at[d - 1], device(me, z=d))
        c.start()
        outs.append(c)
    fin[me["z"]] = fout[me["z"]]
    for d in (1, 3, 2):
        there = fin.at[(me["z"] - d) % 4]
        remote(there, there, fs.at[d - 1], fr.at[d - 1], device(me, k=1)).wait_recv()
    for c in outs:
        c.wait_send()
    for z in range(4):
        f = fin[z].astype(F32)
        rows = jnp.concatenate([f[4 * q : 4 * q + 4] for q in range(4)], axis=1).astype(BF16)
        o_ref[0, :, 1536 * z : 1536 * z + 1536] = rows[0:2]
        o_ref[1, :, 1536 * z : 1536 * z + 1536] = rows[2:4]


ANY = pl.BlockSpec(memory_space=pl.ANY)
VM = pl.BlockSpec(memory_space=pltpu.VMEM)
SM = pl.BlockSpec(memory_space=pltpu.SMEM)
DMA = pltpu.SemaphoreType.DMA


def on_device(hidden_in, queries, new_kv, kv_pool, block_table, cached_len, w_out, norm_gain, expert_ids, expert_gates,
              w_gate, w_up, w_down):
    V = pltpu.VMEM
    return pl.pallas_call(
        layer_kernel,
        out_shape=jax.ShapeDtypeStruct((2, 2, 6144), BF16),
        in_specs=[VM, SM, SM, SM, VM, VM, VM, VM] + [ANY] * 5,
        out_specs=VM,
        scratch_shapes=[
            V((4, 2, 4, 4, 208, 128), BF16), V((4, 2, 4, 4, 192, 128), BF16), V((32, 16, 2048), BF16), V((32, 128, 128), BF16),
            V((384, 6144), BF16), V((6144, 512), BF16), V((6144, 512), BF16), V((512, 6144), BF16),
            V((36, 128, 192), F32), V((36, 1, 192), F32), V((36, 1, 192), F32),
            V((36, 3, 64, 128), BF16), V((36, 3, 1, 128), F32), V((36, 3, 1, 128), F32),
            V((3, 2, 4, 2, 2, 8, 128), F32), V((3, 4, 2, 2, 8, 128), F32), V((4, 4, 4, 192, 128), BF16),
            V((3, 2, 2, 4, 64, 128), BF16), V((3, 2, 4, 2, 64, 128), BF16), V((3, 2, 4, 4, 64, 128), BF16),
            V((3, 3, 4, 64, 128), BF16), V((3, 3, 64, 128), BF16),
            V((3, 2, 2, 8, 128), F32), V((3, 2, 2, 2, 8, 128), F32), V((3, 4, 8, 128), F32), V((3, 3, 8, 128), F32), V((3, 4, 8, 128), F32), V((3, 3, 8, 128), F32),
            V((4, 8, 128), F32), V((192, 128), F32), V((2, 16, 128), F32), V((2, 16, 128), F32), V((48, 128), F32),
            V((40, 256), jnp.int32), V((8, 256), jnp.int32), pltpu.SMEM((8, 256), jnp.int32),
            V((16, 16, 128), BF16), V((16, 16, 128), BF16),
            V((4, 4, 16, 1536), BF16), V((16, 16, 1536), BF16), V((16, 1536), F32), V((4, 16, 384), BF16), V((4, 16, 384), BF16),
            V((4, 2, 4, 16, 1024), F32), V((4, 2, 4, 16, 512), BF16), V((2, 4, 2, 4, 16, 128), F32), V((16, 1536), BF16),
            V((4, 16, 384), BF16), V((4, 16, 384), BF16),
            DMA((6,)), DMA((3, 12)), DMA((3, 12)), DMA((3, 4)), DMA((3, 4)), DMA((3, 12)), DMA((3, 12)), DMA((3, 12)), DMA((3, 12)),
            DMA((3,)), DMA((3,)), DMA((3,)), DMA((3,)), DMA((3,)), DMA((3,)), DMA((16,)), DMA((16,)), DMA((16,)), DMA((16,)),
            DMA((3, 12)), DMA((3, 12)), DMA((3, 4)), DMA((3, 4)), DMA((3, 12)), DMA((3, 12)), DMA((3,)), DMA((3,)), DMA((3,)), DMA((3,)),
        ],
        compiler_params=pltpu.CompilerParams(collective_id=0, has_side_effects=True, vmem_limit_bytes=63 * 2**20),
    )(block_table.T, cached_len, expert_ids, expert_gates, queries, new_kv, hidden_in, norm_gain.reshape(48, 128),
      kv_pool, w_out, w_gate, w_up, w_down)


def solution(mesh):
    both = ("row", "col")
    return jax.shard_map(
        on_device,
        mesh=mesh,
        in_specs=(P(both, None, None), P(both, None, None), P(both, None, None), P(both, None, None), P(), P(), P("col", None),
                  P(), P(both, None, None), P(both, None, None), P("row", None, "col"), P("row", None, "col"), P("row", "col", None)),
        out_specs=P(both, None, None),
        check_vma=False,
    )
```

```python
import jax, functools
import jax.numpy as jnp
from jax import lax
from jax.experimental import pallas as pl
from jax.experimental.pallas import tpu as pltpu
from jax.sharding import PartitionSpec as P

MESH = pl.DeviceIdType.MESH
ORDERS = (("x", "y", "z"), ("y", "z", "x"), ("z", "x", "y"))
F32, BF16 = jnp.float32, jnp.bfloat16


def where_am_i():
    r, c = lax.axis_index("row"), lax.axis_index("col")
    return {"y": lax.div(r, 2), "k": lax.rem(r, 2), "x": lax.div(c, 4), "z": lax.rem(c, 4)}


def turned(v, step):
    return lax.rem(v + (step + 4), 4)


def device(me, **moved):
    at = dict(me)
    for name, step in moved.items():
        at[name] = lax.rem(me[name] + step, 2) if name == "k" else turned(me[name], step)
    return (at["y"] * 2 + at["k"], at["x"] * 4 + at["z"])


def pick(sel, name):
    return sel.get(name, slice(None))


def block_of(ref, k, sel, part):
    return ref.at[(pick(sel, "y"), k, pick(sel, "x"), pick(sel, "z")) + part]


def remote(src, dst, send, recv, where):
    return pltpu.make_async_remote_copy(
        src_ref=src, dst_ref=dst, send_sem=send, recv_sem=recv, device_id=where, device_id_type=MESH
    )


def greet(me, plane=False):
    bar = pltpu.get_barrier_semaphore()
    count = 0
    for name in ("x", "y", "z"):
        for d in (1, 2, 3):
            pl.semaphore_signal(bar, inc=1, device_id=device(me, **{name: d}), device_id_type=MESH)
            count += 1
    pl.semaphore_signal(bar, inc=1, device_id=device(me, k=1), device_id_type=MESH)
    count += 1
    if plane:
        for dx in (1, 2, 3):
            for dz in (1, 2, 3):
                pl.semaphore_signal(bar, inc=1, device_id=device(me, x=dx, z=dz), device_id_type=MESH)
                count += 1
    pl.semaphore_wait(bar, count)


def shift(me, **moved):
    return {n: turned(me[n], -s) for n, s in moved.items()}


HALF = (slice(0, 2), slice(2, 4))


def gather_blocks(buf, me, parts, send, recv, cs, cr, hooks=(), on_line=None):
    k = me["k"]
    started = []

    def go(p, sel, moved, i):
        there = block_of(buf, k, sel, parts[p])
        copy = remote(there, there, send.at[p, i], recv.at[p, i], device(me, **moved))
        copy.start()
        started.append(copy)

    def landed(p, sel, i):
        here = block_of(buf, k, sel, parts[p])
        remote(here, here, send.at[p, i], recv.at[p, i], device(me, k=1)).wait_recv()

    def across(p, sel, i, kk=k):
        there = block_of(buf, kk, sel, parts[p])
        return remote(there, there, cs.at[p, i], cr.at[p, i], device(me, k=1))

    def cross(p, sel, i):
        copy = across(p, sel, i)
        copy.start()
        started.append(copy)

    for p, (a, b, c) in enumerate(ORDERS):
        for d in (2, 1, 3):
            go(p, {n: me[n] for n in "xyz"}, {a: d}, d - 1)
    if hooks:
        hooks[0]()
    for p, (a, b, c) in enumerate(ORDERS):
        for d in (1, 3, 2):
            landed(p, {a: turned(me[a], -d), b: me[b], c: me[c]}, d - 1)
        for d in (2, 1, 3):
            go(p, {b: me[b], c: me[c]}, {b: d}, 3 + d - 1)
    if hooks:
        hooks[1]()
    for p, (a, b, c) in enumerate(ORDERS):
        for d in (1, 3, 2):
            landed(p, {b: turned(me[b], -d), c: me[c]}, 3 + d - 1)
        go(p, {b: HALF[0], c: me[c]}, {c: 1}, 6)
        go(p, {b: HALF[1], c: me[c]}, {c: -1}, 9)
        go(p, {b: HALF[1], c: me[c]}, {c: 1}, 7)
        go(p, {b: HALF[0], c: me[c]}, {c: -1}, 8)
        cross(p, {c: me[c]}, 0)
    if hooks:
        hooks[2]()

    def both_cores(i, d):
        for p, (a, b, c) in enumerate(ORDERS):
            across(p, {c: turned(me[c], d)}, i, 1 - k).wait_recv()
        if on_line:
            on_line(d)

    both_cores(0, 0)
    for p, (a, b, c) in enumerate(ORDERS):
        landed(p, {b: HALF[0], c: turned(me[c], -1)}, 6)
        go(p, {b: HALF[0], c: turned(me[c], -1)}, {c: 1}, 10)
        landed(p, {b: HALF[1], c: turned(me[c], 1)}, 9)
        go(p, {b: HALF[1], c: turned(me[c], 1)}, {c: -1}, 11)
    for p, (a, b, c) in enumerate(ORDERS):
        landed(p, {b: HALF[1], c: turned(me[c], -1)}, 7)
        cross(p, {c: turned(me[c], -1)}, 1)
        landed(p, {b: HALF[0], c: turned(me[c], 1)}, 8)
        cross(p, {c: turned(me[c], 1)}, 2)
    both_cores(1, 3)
    both_cores(2, 1)
    for p, (a, b, c) in enumerate(ORDERS):
        landed(p, {b: HALF[0], c: turned(me[c], 2)}, 10)
        landed(p, {b: HALF[1], c: turned(me[c], 2)}, 11)
        cross(p, {c: turned(me[c], 2)}, 3)
    both_cores(3, 2)
    for copy in started:
        copy.wait_send()


def send_core(buf, me, parts, core, cs, cr, p):
    copy = remote(
        buf.at[(slice(None), 1 - me["k"], slice(None), slice(None)) + parts[p]],
        core.at[(slice(None), slice(None), slice(None)) + parts[p]],
        cs.at[p], cr.at[p], device(me, k=1),
    )
    copy.start()
    return copy


def scatter_blocks(buf, me, parts, fwd, line, r2, r3, send, recv, started, ready):
    k = me["k"]

    def go(p, sel, moved, dst, i):
        copy = remote(block_of(buf, k, sel, parts[p]), dst, send.at[p, i], recv.at[p, i], device(me, **moved))
        copy.start()
        started.append(copy)

    def landed(p, dst, i):
        remote(dst, dst, send.at[p, i], recv.at[p, i], device(me, k=1)).wait_recv()

    def rest_of(c):
        return [n for n in ("y", "x", "z") if n != c]

    def sub(ref, p, j, b, c, half):
        return ref.at[(p, j) + tuple(HALF[half] if n == b else slice(None) for n in rest_of(c))]

    def add(p, b, c, at, half, terms):
        rest = rest_of(c)

        for n in range(8):
            i_b, i_a = 2 * half + n // 4, n % 4
            idx = {c: at, **{m: (i_b if m == b else i_a) for m in rest}}
            mine = (idx["y"], k, idx["x"], idx["z"]) + parts[p]
            total = buf[mine].astype(F32)
            for t in terms:
                total += t(idx, rest, n).astype(F32)
            buf[mine] = total.astype(BF16)

    for p, (a, b, c) in enumerate(ORDERS):
        ready(p)
        far, right, left = turned(me[c], 2), turned(me[c], 1), turned(me[c], -1)
        go(p, {c: far, b: HALF[0]}, {c: 1}, fwd_dst(fwd, p, 0, a, b, c), 0)
        go(p, {c: far, b: HALF[1]}, {c: -1}, fwd_dst(fwd, p, 1, a, b, c), 1)
        go(p, {c: right, b: HALF[1]}, {c: 1}, sub(line, p, 0, b, c, 1), 2)
        go(p, {c: left, b: HALF[0]}, {c: -1}, sub(line, p, 1, b, c, 0), 3)
    for p, (a, b, c) in enumerate(ORDERS):
        right, left = turned(me[c], 1), turned(me[c], -1)
        landed(p, fwd_dst(fwd, p, 0, a, b, c), 0)
        add(p, b, c, right, 0, [fwd_at(fwd, p, 0, a, b, c)])
        go(p, {c: right, b: HALF[0]}, {c: 1}, sub(line, p, 0, b, c, 0), 4)
        landed(p, fwd_dst(fwd, p, 1, a, b, c), 1)
        add(p, b, c, left, 1, [fwd_at(fwd, p, 1, a, b, c)])
        go(p, {c: left, b: HALF[1]}, {c: -1}, sub(line, p, 1, b, c, 1), 5)
    for p, (a, b, c) in enumerate(ORDERS):
        for i, (j, h) in ((2, (0, 1)), (3, (1, 0)), (4, (0, 0)), (5, (1, 1))):
            landed(p, sub(line, p, j, b, c, h), i)
        def lt(j, p=p):
            return lambda idx, rest, n: line[p, j, idx[rest[0]], idx[rest[1]]]
        for h in range(2):
            add(p, b, c, me[c], h, [lt(0), lt(1)])
        for d in (2, 1, 3):
            go(p, {c: me[c], b: turned(me[b], d)}, {b: d}, r2.at[p, d - 1], 5 + d)
    for p, (a, b, c) in enumerate(ORDERS):
        for d in (1, 2, 3):
            landed(p, r2.at[p, d - 1], 5 + d)
        for i in range(4):
            idx = {c: me[c], b: me[b], a: i}
            mine = (idx["y"], k, idx["x"], idx["z"]) + parts[p]
            total = buf[mine].astype(F32)
            for d in range(3):
                total += r2[p, d, i].astype(F32)
            buf[mine] = total.astype(BF16)
        for d in (2, 1, 3):
            go(p, {c: me[c], b: me[b], a: turned(me[a], d)}, {a: d}, r3.at[p, d - 1], 8 + d)
    sums = []
    for p, (a, b, c) in enumerate(ORDERS):
        for d in (1, 2, 3):
            landed(p, r3.at[p, d - 1], 8 + d)
        total = buf[(me["y"], k, me["x"], me["z"]) + parts[p]].astype(F32)
        for d in range(3):
            total += r3[p, d].astype(F32)
        sums.append(total)
    for copy in started:
        copy.wait_send()
    return sums


def half_first(a, b, c):
    rest = [n for n in ("y", "x", "z") if n != c]
    return rest[0] == b


def fwd_dst(fwd, p, j, a, b, c):
    return fwd[half_first(a, b, c)].at[p, j]


def fwd_at(fwd, p, j, a, b, c):
    if half_first(a, b, c):
        return lambda idx, rest, n: fwd[True][p, j, n // 4, n % 4]
    return lambda idx, rest, n: fwd[False][p, j, n % 4, n // 4]


QPARTS = [(slice(64 * p, 64 * p + 64), slice(None)) for p in range(3)]
EMPTY = 34


def layer_kernel(table, clen, ids, gates, queries, new_kv, hidden, gain, kv_h, wo_h, wg_h, wu_h, wd_h, o_ref,
                 X, A, KV, VT, WO, WG, WU, WD, accs, ms, ls, ms2, ls2, Z, Zm, Zl, PI, PM, St, Cst, core, fa, fb, line, r2, r3, sf, sl, St2, s2, St3, s3,
                 U, NK, NV, GF, CC, info_v, info, G, H, O, Rv, hid, hin, hrec, acc, act, scal, resid, fout, fin,
                 lsem, gs, gr, gcs, gcr, ss_, sr, ts, tr, scs, scr, tcs, tcr, hs, hr, as_, ar, ps, pr,
                 gs2, gr2, gcs2, gcr2, ss2, sr2, scs2, scr2, fs, fr):
    me = where_am_i()
    k = me["k"]
    rank = me["y"] * 32 + k * 16 + me["x"] * 4 + me["z"]
    kv_load = pltpu.make_async_copy(kv_h, KV, lsem.at[0])
    wo_load = pltpu.make_async_copy(wo_h, WO, lsem.at[1])
    loads = [pltpu.make_async_copy(h.at[0], v, lsem.at[2 + i]) for i, (h, v) in enumerate(((wg_h, WG), (wu_h, WU), (wd_h, WD)))]
    info_load = pltpu.make_async_copy(info_v, info, lsem.at[5])
    kv_load.start()
    wo_load.start()
    for c in loads:
        c.start()
    for i in range(2):
        q = queries[i].astype(F32)
        for h in range(48):
            U[pl.ds((h // 16) * 64 + i * 32 + h % 16, 2, stride=16), :] = q[:, 128 * h : 128 * h + 128]
    X[me["y"], k, me["x"], me["z"], 0:192, :] = U[...].astype(BF16)
    greet(me, plane=True)
    started = []

    def find_blocks():
        code = lax.broadcasted_iota(jnp.int32, (64, 256), 1) * 64 + lax.broadcasted_iota(jnp.int32, (64, 256), 0)

        def search(j, _):
            CC[pl.ds(j, 1), :] = jnp.max(jnp.where(table[...] == rank * 32 + j, code, -1), axis=0, keepdims=True)
            return 0

        lax.fori_loop(0, 32, search, 0, unroll=4)
        CC[32:40, :] = jnp.full((8, 256), -1, jnp.int32)
        found = jnp.max(CC[...], axis=1, keepdims=True)
        r = lax.broadcasted_iota(jnp.int32, (40, 128), 0)
        c = lax.broadcasted_iota(jnp.int32, (40, 128), 1)
        found = jnp.broadcast_to(found, (40, 128))
        found = jnp.where((r == 32) | (r == 33), (rank * 2 + r - 32) * 64, found)
        owner = jnp.where(found >= 0, found // 64, -1)
        as_row = lambda v: jnp.max(jnp.where(r == c, v, -1), axis=0, keepdims=True)
        PI[...] = jnp.where(r == 35, 1, jnp.where(owner < 0, 0, owner % 2))
        owner_row, place_row = as_row(owner), as_row(jnp.where(found >= 0, found % 64, 0))
        before = jnp.max(jnp.where((owner == owner_row) & (r < c) & (owner >= 0), r, -1), axis=0, keepdims=True)
        info_v[1:2, 0:128] = jnp.where(before < 0, EMPTY, before)
        cr = c[0:1]
        info_v[2:3, 0:128] = jnp.where(cr < 34, jnp.maximum(owner_row, 0), jnp.where(cr == 35, 1, 0))
        info_v[3:4, 0:128] = jnp.maximum(place_row, 0)
        r2_ = lax.broadcasted_iota(jnp.int32, (40, 256), 0)
        c2_ = lax.broadcasted_iota(jnp.int32, (40, 256), 1)
        owner2 = jnp.concatenate([owner, owner], axis=1)
        last_ = jnp.max(jnp.where(owner2 == c2_, r2_, -1), axis=0, keepdims=True)
        info_v[0:1, :] = jnp.where(last_ < 0, EMPTY + c2_[0:1] % 2, last_)
        info_load.start()

    def small_things():
        for i in range(2):
            v = new_kv[i].astype(F32)
            for g in range(8):
                NK[i, 2 * g : 2 * g + 2, :] = v[:, 128 * g : 128 * g + 128]
                NV[i, 2 * g : 2 * g + 2, :] = v[:, 1024 + 128 * g : 1152 + 128 * g]
        GF[...] = gain[...].astype(F32)
        f = jnp.concatenate([hidden[0].astype(F32), hidden[1].astype(F32)], axis=0)
        for z in range(4):
            hin[z] = jnp.concatenate([f[:, 1536 * z + 384 * q : 1536 * z + 384 * q + 384] for q in range(4)], axis=0).astype(BF16)
        for d in (1, 2, 3):
            c = remote(hin.at[turned(me["z"], d)], hrec.at[me["z"]], hs.at[d - 1], hr.at[d - 1], device(me, z=d))
            c.start()
            started.append(c)
        hrec[me["z"]] = hin[me["z"]]

    def turn_values():
        kv_load.wait()

        def turn(j, _):
            v = jnp.concatenate([KV[j, :, 1024 + 128 * g : 1152 + 128 * g] for g in range(8)], axis=0)
            VT[j] = v.astype(F32).T.astype(BF16)
            return 0

        lax.fori_loop(0, 32, turn, 0, unroll=4)
        fresh_slots()

    lane = lax.broadcasted_iota(jnp.int32, (128, 128), 1)
    rowi = lax.broadcasted_iota(jnp.int32, (128, 128), 0)
    head_kv = jnp.where(lane < 96, ((lane // 32) * 16 + lane % 16) // 6, -1)
    lane_s = (lane // 16) % 2
    same = jnp.where(head_kv == rowi // 16, rowi % 16, 99)
    to_bits = 128 ** -0.5 * 1.4426950408889634

    def query_rows(at, i):
        first = jnp.broadcast_to(jnp.asarray(i, jnp.int32), (32, 128)) == 0
        pieces = []
        for p in (0, 1, 2):
            a, b = (X[at + (slice(64 * p + o, 64 * p + o + 32), slice(None))].astype(F32) for o in (0, 32))
            pieces.append(jnp.where(first, a, b).astype(BF16))
        return jnp.concatenate(pieces + pieces[:1], axis=0)

    def attend(st, ok, vt, j):
        st = jnp.where(ok, st, -1e30)
        m = jnp.max(st, axis=0, keepdims=True)
        w = jnp.exp2((st - m) * to_bits)
        accs[j] = jnp.dot(vt, w.astype(BF16), preferred_element_type=F32)
        ms[j] = m * to_bits
        ls[j] = jnp.sum(w, axis=0, keepdims=True)

    def fresh_slots():
        r = rowi[:16]
        for i in range(32, 36):
            ms[i] = jnp.full((1, 128), -1e30, F32)
            ls[i] = jnp.zeros((1, 128), F32)
        ms2[32:40, :] = jnp.full((8, 128), -1e30, F32)
        ls2[32:40, :] = jnp.zeros((8, 128), F32)
        row2 = lax.broadcasted_iota(jnp.int32, (256, 384), 0)
        col2 = lax.broadcasted_iota(jnp.int32, (256, 384), 1)
        source = (col2 % 128) // 64 * 128 + col2 // 128 * 32 + col2 % 32
        for i in range(2):
            PM[i] = jnp.where((row2 == source) & ((col2 // 32) % 2 == i), 1.0, 0.0).astype(BF16)
            own = query_rows((me["y"], k, me["x"], me["z"]), i)
            st = lax.dot_general(NK[i].astype(BF16), own, (((1,), (1,)), ((), ())), preferred_element_type=F32)
            attend(st, (head_kv[:16] == r // 2) & (r % 2 <= lane_s[:16]), NV[i].T.astype(BF16), 32 + i)
            accs[EMPTY + i] = jnp.zeros((128, 128), F32)

    gather_blocks(X, me, QPARTS, gs, gr, gcs, gcr, (find_blocks, small_things, turn_values))
    info_load.wait()

    def score(j, _):
        rq = info[2, j]
        q = query_rows((lax.div(rq, 64), lax.rem(lax.div(rq, 32), 2), lax.rem(lax.div(rq, 8), 4), lax.rem(lax.div(rq, 2), 4)), lax.rem(rq, 2))
        ks = jnp.concatenate([KV[j, :, 128 * g : 128 * g + 128] for g in range(8)], axis=0)
        accs[j] = lax.dot_general(ks, q, (((1,), (1,)), ((), ())), preferred_element_type=F32)
        return 0

    def weigh(j, _):
        seen = jnp.clip(clen[info[2, j]] - 16 * info[3, j], 0, 16)
        st = jnp.where(same < seen, accs[j], -1e30)
        m = jnp.max(st, axis=0, keepdims=True)
        w = jnp.exp2((st - m) * to_bits)
        ms[j] = m * to_bits
        ls[j] = jnp.sum(w, axis=0, keepdims=True)
        Z[j, 0] = w[:64].astype(BF16)
        Z[j, 1] = w[64:].astype(BF16)
        return 0

    def mix(j, _):
        accs[j] = jnp.dot(VT[j], jnp.concatenate([Z[j, 0], Z[j, 1]], axis=0), preferred_element_type=F32)
        return 0

    lax.fori_loop(0, 32, score, 0, unroll=8)
    lax.fori_loop(0, 32, weigh, 0, unroll=4)
    lax.fori_loop(0, 32, mix, 0, unroll=8)
    def chain(j, _):
        pj = info[1, j]
        m0, m1 = ms[j], ms[pj]
        m = jnp.maximum(m0, m1)
        w0, w1 = jnp.exp2(m0 - m), jnp.exp2(m1 - m)
        l = ls[j] * w0 + ls[pj] * w1
        accs[j] = accs[j] * w0 + accs[pj] * w1
        ls[j] = l
        ms[j] = m
        ms2[pl.ds(j, 1), :] = m
        ls2[pl.ds(j, 1), :] = l
        return 0

    def put(j, _):
        both = jnp.concatenate([accs[j, 0:64, :], accs[j, 64:128, :]], axis=1).astype(BF16)
        t = jnp.dot(both, PM[lax.rem(info[2, j], 2)], preferred_element_type=F32).astype(BF16)
        for p in range(3):
            Z[j, p] = t[:, 128 * p : 128 * p + 128]
        return 0

    lax.fori_loop(0, 34, chain, 0, unroll=2)
    lax.fori_loop(0, 36, put, 0, unroll=6)
    ln = lane[:40]
    for v, Zv in ((ms2, Zm), (ls2, Zl)):
        for p in range(3):
            t = jnp.where(ln < 64, pltpu.roll(v[...], (128 - 32 * p) % 128, 1), pltpu.roll(v[...], (192 - 32 * p) % 128, 1))
            t = jnp.where(ln % 64 < 32, t, 0.0)
            t = jnp.where(PI[...] == 0, t, pltpu.roll(t, 32, 1))
            for j in range(36):
                Zv[p, j] = t[j : j + 1]
    def spread(kk, ps_):
        def body(y, _):
            for x in range(4):
                for z in range(4):
                    to = y * 32 + kk * 16 + x * 4 + z
                    s0, s1_ = info[0, 2 * to], info[0, 2 * to + 1]
                    for p in ps_:
                        A[y, kk, x, z, 64 * p : 64 * p + 64, :] = Z[s0, p] + Z[s1_, p]
                        m, l = (Zv[p, s0] + Zv[p, s1_] for Zv in (Zm, Zl))
                        if p == 0:
                            at = (z, lax.div(y, 2), pl.ds(lax.rem(y, 2) * 4 + x, 1))
                        elif p == 1:
                            at = (x, z // 2, pl.ds((z % 2) * 4 + y, 1))
                        else:
                            at = (y, x // 2, slice((x % 2) * 4 + z, (x % 2) * 4 + z + 1))
                        St[(p, kk) + at[:2] + (0, at[2], slice(None))] = m
                        St[(p, kk) + at[:2] + (1, at[2], slice(None))] = l
            return 0

        lax.fori_loop(0, 4, body, 0)

    cores = []
    for p in range(3):
        spread(1 - k, (p,))
        c0 = send_core(A, me, QPARTS, core, scs, scr, p)
        c1 = remote(St.at[p, 1 - k], Cst.at[p], tcs.at[p], tcr.at[p], device(me, k=1))
        c1.start()
        cores.append((c0, c1))
        started.extend((c0, c1))
    spread(k, (0, 1, 2))

    def go(p, sel, moved, dst, i, stat, sdst):
        c0 = remote(block_of(A, k, sel, QPARTS[p]), dst, ss_.at[p, i], sr.at[p, i], device(me, **moved))
        c1 = remote(stat, sdst, ts.at[p, i], tr.at[p, i], device(me, **moved))
        c0.start()
        c1.start()
        started.extend((c0, c1))

    def landed(p, dst, i, sdst):
        remote(dst, dst, ss_.at[p, i], sr.at[p, i], device(me, k=1)).wait_recv()
        remote(sdst, sdst, ts.at[p, i], tr.at[p, i], device(me, k=1)).wait_recv()

    def merge(stats):
        top = functools.reduce(jnp.maximum, [m for m, _ in stats])
        ws = [jnp.exp2(m - top) for m, _ in stats]
        return top, sum(w * l for w, (_, l) in zip(ws, stats)), ws

    def others(c):
        return [n for n in ("y", "x", "z") if n != c]

    fwd = {True: fa, False: fb}

    def half_line(p, j, b, c, h):
        return line.at[(p, j) + tuple(HALF[h] if n == b else slice(None) for n in others(c))]

    def blend(p, at, h, sources):
        a, b, c = ORDERS[p]
        here = St[p, k, at, h]
        stats = [(here[0], here[1])] + [(s[0], s[1]) for _, s in sources]
        top, tot, ws = merge(stats)
        St[p, k, at, h, 0] = top
        St[p, k, at, h, 1] = tot
        for n in range(8):
            idx = {c: at, b: 2 * h + n // 4, a: n % 4}
            mine = (idx["y"], k, idx["x"], idx["z"]) + QPARTS[p]
            t = A[mine].astype(F32) * ws[0][n : n + 1]
            for i, (block, _) in enumerate(sources):
                t += block(idx, n).astype(F32) * ws[i + 1][n : n + 1]
            A[mine] = t.astype(BF16)

    def from_core(p, at, h):
        return (lambda idx, n: core[(idx["y"], idx["x"], idx["z"]) + QPARTS[p]]), Cst[p, at, h]

    def from_fwd(p, j):
        a, b, c = ORDERS[p]
        get = fwd_at(fwd, p, j, a, b, c)
        return (lambda idx, n: get(idx, None, n)), sf[p, j]

    def from_line(p, j, h):
        rest = others(ORDERS[p][2])
        return (lambda idx, n: line[p, j, idx[rest[0]], idx[rest[1]]]), sl[p, j, h]

    for p, (a, b, c) in enumerate(ORDERS):
        for copy in cores[p]:
            copy.wait_recv()
        far, right, left = turned(me[c], 2), turned(me[c], 1), turned(me[c], -1)
        blend(p, far, 0, [from_core(p, far, 0)])
        go(p, {c: far, b: HALF[0]}, {c: 1}, fwd_dst(fwd, p, 0, a, b, c), 0, St.at[p, k, far, 0], sf.at[p, 0])
        blend(p, far, 1, [from_core(p, far, 1)])
        go(p, {c: far, b: HALF[1]}, {c: -1}, fwd_dst(fwd, p, 1, a, b, c), 1, St.at[p, k, far, 1], sf.at[p, 1])
        blend(p, right, 1, [from_core(p, right, 1)])
        go(p, {c: right, b: HALF[1]}, {c: 1}, half_line(p, 0, b, c, 1), 2, St.at[p, k, right, 1], sl.at[p, 0, 1])
        blend(p, left, 0, [from_core(p, left, 0)])
        go(p, {c: left, b: HALF[0]}, {c: -1}, half_line(p, 1, b, c, 0), 3, St.at[p, k, left, 0], sl.at[p, 1, 0])
    for p, (a, b, c) in enumerate(ORDERS):
        right, left = turned(me[c], 1), turned(me[c], -1)
        landed(p, fwd_dst(fwd, p, 0, a, b, c), 0, sf.at[p, 0])
        blend(p, right, 0, [from_core(p, right, 0), from_fwd(p, 0)])
        go(p, {c: right, b: HALF[0]}, {c: 1}, half_line(p, 0, b, c, 0), 4, St.at[p, k, right, 0], sl.at[p, 0, 0])
        landed(p, fwd_dst(fwd, p, 1, a, b, c), 1, sf.at[p, 1])
        blend(p, left, 1, [from_core(p, left, 1), from_fwd(p, 1)])
        go(p, {c: left, b: HALF[1]}, {c: -1}, half_line(p, 1, b, c, 1), 5, St.at[p, k, left, 1], sl.at[p, 1, 1])
    for p, (a, b, c) in enumerate(ORDERS):
        for h in range(2):
            blend(p, me[c], h, [from_core(p, me[c], h)])
    for p, (a, b, c) in enumerate(ORDERS):
        for i, (j, h) in ((2, (0, 1)), (3, (1, 0)), (4, (0, 0)), (5, (1, 1))):
            landed(p, half_line(p, j, b, c, h), i, sl.at[p, j, h])
        for h in range(2):
            blend(p, me[c], h, [from_line(p, 0, h), from_line(p, 1, h)])
            for i in range(2):
                St2[p, 2 * h + i, 0:4] = St[p, k, me[c], h, 0, 4 * i : 4 * i + 4]
                St2[p, 2 * h + i, 4:8] = St[p, k, me[c], h, 1, 4 * i : 4 * i + 4]
        for d in (2, 1, 3):
            at = turned(me[b], d)
            go(p, {c: me[c], b: at}, {b: d}, r2.at[p, d - 1], 5 + d, St2.at[p, at], s2.at[p, d - 1])
    for p, (a, b, c) in enumerate(ORDERS):
        for d in (1, 2, 3):
            landed(p, r2.at[p, d - 1], 5 + d, s2.at[p, d - 1])
        stats = [St2[p, me[b]]] + [s2[p, d] for d in range(3)]
        top, tot, ws = merge([(s[0:4], s[4:8]) for s in stats])
        for i in range(4):
            idx = {c: me[c], b: me[b], a: i}
            mine = (idx["y"], k, idx["x"], idx["z"]) + QPARTS[p]
            t = A[mine].astype(F32) * ws[0][i : i + 1]
            for d in range(3):
                t += r2[p, d, i].astype(F32) * ws[d + 1][i : i + 1]
            A[mine] = t.astype(BF16)
            St3[p, i, 0:1] = top[i : i + 1]
            St3[p, i, 1:2] = tot[i : i + 1]
        for d in (2, 1, 3):
            at = turned(me[a], d)
            go(p, {c: me[c], b: me[b], a: at}, {a: d}, r3.at[p, d - 1], 8 + d, St3.at[p, at], s3.at[p, d - 1])
    for p, (a, b, c) in enumerate(ORDERS):
        for d in (1, 2, 3):
            landed(p, r3.at[p, d - 1], 8 + d, s3.at[p, d - 1])
        stats = [St3[p, me[a]]] + [s3[p, d] for d in range(3)]
        top, tot, ws = merge([(s[0:1], s[1:2]) for s in stats])
        t = A[(me["y"], k, me["x"], me["z"]) + QPARTS[p]].astype(F32) * ws[0]
        for d in range(3):
            t += r3[p, d].astype(F32) * ws[d + 1]
        t = t / tot
        both = jnp.concatenate([t, pltpu.roll(t, 64, 1)], axis=0)
        U[64 * p : 64 * p + 64, :] = both.T[:64]
    for c in range(16):
        rows = []
        for hh in range(3):
            h = 3 * c + hh
            rows.append(U[pl.ds((h // 16) * 64 + h % 16, 4, stride=16), :])
        G[c] = jnp.concatenate(rows + [jnp.zeros((4, 128), F32)], axis=0).astype(BF16)
    col = me["x"] * 4 + me["z"]
    steps = [(dx, dz) for dz in (2, 1, 3, 0) for dx in (2, 1, 3, 0) if dx or dz]

    def peer(dx, dz):
        return (turned(me["x"], dx)) * 4 + turned(me["z"], dz)

    for dx, dz in steps:
        c = remote(G.at[peer(dx, dz)], H.at[col], as_.at[dx * 4 + dz], ar.at[dx * 4 + dz], device(me, x=dx, z=dz))
        c.start()
        started.append(c)
    H[col] = G[col]
    for d in (1, 2, 3):
        there = hrec.at[turned(me["z"], -d)]
        remote(there, there, hs.at[d - 1], hr.at[d - 1], device(me, k=1)).wait_recv()
    for z in range(4):
        f = hrec[z].astype(F32)
        hid[4 * z : 4 * z + 4, :] = jnp.concatenate([f[4 * q : 4 * q + 4] for q in range(4)], axis=1)
    wo_load.wait()
    for dx, dz in steps:
        there = H.at[peer(-dx, -dz)]
        remote(there, there, as_.at[dx * 4 + dz], ar.at[dx * 4 + dz], device(me, k=1)).wait_recv()
    heads = []
    hf = [H[c].astype(F32) for c in range(16)]
    for hh in range(3):
        heads.append(jnp.concatenate([hf[c][4 * hh : 4 * hh + 4] for c in range(16)], axis=0).astype(BF16))
    lhs = jnp.concatenate(heads, axis=1)
    for dz in (2, 1, 3, 0):
        zz = turned(me["z"], dz)
        res = jnp.dot(lhs, WO[:, pl.ds(pl.multiple_of(zz * 1536, 1536), 1536)], preferred_element_type=F32).astype(BF16)
        for x in range(4):
            O[x, zz] = res[16 * x : 16 * x + 16]
        for dx in (2, 1, 3, 0):
            if dx or dz:
                c = remote(O.at[turned(me["x"], dx), zz], Rv.at[col], ps.at[dx * 4 + dz], pr.at[dx * 4 + dz], device(me, x=dx, z=dz))
                c.start()
                started.append(c)
    Rv[col] = O[me["x"], me["z"]]
    for dx, dz in steps:
        there = Rv.at[peer(-dx, -dz)]
        remote(there, there, ps.at[dx * 4 + dz], pr.at[dx * 4 + dz], device(me, k=1)).wait_recv()
    total = Rv[0].astype(F32)
    for c in range(1, 16):
        total += Rv[c].astype(F32)
    res = (hid[...] + total).astype(BF16)
    resid[...] = res
    f = res.astype(F32)
    xg = jnp.concatenate([f[:, 128 * c : 128 * c + 128] * GF[pl.ds(me["z"] * 12 + c, 1), :] for c in range(12)], axis=1).astype(BF16)
    squares = jnp.sum(f * f, axis=1, keepdims=True)
    high = squares.astype(BF16).astype(F32)
    low = squares - high
    ln = lax.broadcasted_iota(jnp.int32, (16, 128), 1)
    rw = lax.broadcasted_iota(jnp.int32, (16, 128), 0)
    gt = jnp.zeros((16, 128), F32)
    for t in range(4):
        for n in range(2):
            gt += jnp.where((rw == 4 * me["z"] + t) & (ln == 8 + ids[t // 2, t % 2, n]), gates[t // 2, t % 2, n], 0.0)
    gh = gt.astype(BF16).astype(F32)
    tile = gh + pltpu.roll(gt - gh, 8, 1)
    tile = jnp.where(ln == 0, high, jnp.where(ln == 1, low, tile)).astype(BF16)
    here = (me["y"], k, me["x"], me["z"])
    for c in range(12):
        X[here + (slice(16 * c, 16 * c + 16), slice(None))] = xg[:, 128 * c : 128 * c + 128]
    X[here + (slice(192, 208), slice(None))] = tile
    for c in started:
        c.wait_send()
    experts(me, X, WG, WU, WD, A, core, fwd, line, r2, r3, acc, act, scal, resid, fout, fin, loads,
            gs2, gr2, gcs2, gcr2, ss2, sr2, scs2, scr2, fs, fr, o_ref)


XPARTS = [(slice(0, 64), slice(None)), (slice(64, 128), slice(None)), (slice(128, 208), slice(None))]


def experts(me, X, WG, WU, WD, A, core, fwd, line, r2, r3, acc, act, scal, resid, fout, fin, loads,
            gs, gr, gcs, gcr, ss_, sr, scs, scr, fs, fr, o_ref):
    k = me["k"]
    expert = me["y"] * 2 + k
    acc[...] = jnp.zeros_like(acc)

    def add_products(at, terms):
        xs = []
        for rows, z, p in terms:
            x = jnp.concatenate([X[rows + (slice(16 * n, 16 * n + 16), slice(None))] for n in range(4 * p, 4 * p + 4)], axis=-1)
            lead = x.shape[:-1]
            xs.append((x.reshape(-1, 512), pl.ds(pl.multiple_of(z * 1536 + 512 * p, 512), 512)))
        for n, W in enumerate((WG, WU)):
            for h in range(2):
                cols = slice(512 * n + 256 * h, 512 * n + 256 * h + 256)
                r = sum(jnp.dot(x, W[depth, 256 * h : 256 * h + 256], preferred_element_type=F32) for x, depth in xs)
                acc[at + (cols,)] += r.reshape(lead + (256,))

    def on_line(d):
        if d == 0:
            loads[0].wait()
            loads[1].wait()
        full = slice(None)
        z, x, y = turned(me["z"], d), turned(me["x"], d), turned(me["y"], d)
        add_products((full, full, full, full), [((full, full, full, z), z, 0)])
        add_products((full, full, x, full), [((full, full, x, zz), zz, 1) for zz in range(4)])
        add_products((y, full, full, full), [((y, full, full, zz), zz, 2) for zz in range(4)])

    gather_blocks(X, me, XPARTS, gs, gr, gcs, gcr, (), on_line)
    loads[2].wait()
    extra = jnp.zeros((512, 128), F32)
    for z in range(4):
        extra += X[:, :, :, z, 192:208, :].reshape(512, 128).astype(F32)
    lane = lax.broadcasted_iota(jnp.int32, (512, 128), 1)
    squares = jnp.sum(jnp.where(lane < 3, extra, 0.0), axis=1, keepdims=True)
    weight = jnp.sum(jnp.where((lane == 8 + expert) | (lane == 16 + expert), extra, 0.0), axis=1, keepdims=True)
    scal[0] = jnp.broadcast_to(lax.rsqrt(squares * (1.0 / 6144.0) + 1e-5), (512, 128)).reshape(4, 2, 4, 16, 128)
    scal[1] = jnp.broadcast_to(weight, (512, 128)).reshape(4, 2, 4, 16, 128)
    started = []

    def activate(kk):
        at = (slice(None), kk, slice(None), slice(None))
        for n in range(4):
            rs = scal[(0,) + at].reshape(256, 128)
            g = acc[at + (slice(128 * n, 128 * n + 128),)].reshape(256, 128) * rs
            u = acc[at + (slice(512 + 128 * n, 640 + 128 * n),)].reshape(256, 128) * rs
            v = g / (1.0 + jnp.exp(-g)) * u * scal[(1,) + at].reshape(256, 128)
            act[at + (slice(128 * n, 128 * n + 128),)] = v.astype(BF16).reshape(4, 4, 16, 128)

    def down(kk, p, with_core):
        def body(z, _):
            cols = pl.ds(pl.multiple_of(z * 1536 + 512 * p, 512), 512)
            r = jnp.dot(act[:, kk].reshape(256, 512), WD[:, cols], preferred_element_type=F32)
            for n in range(4):
                rows = slice(64 * p + 16 * n, 64 * p + 16 * n + 16)
                t = r[:, 128 * n : 128 * n + 128].reshape(4, 4, 16, 128)
                if with_core:
                    t += core[:, :, z, rows, :].astype(F32)
                A[:, kk, :, z, rows, :] = t.astype(BF16)
            return 0

        lax.fori_loop(0, 4, body, 0)

    activate(1 - k)
    for p in range(3):
        down(1 - k, p, False)
        started.append(send_core(A, me, QPARTS, core, scs, scr, p))
    activate(k)

    def ready(p):
        started[p].wait_recv()
        down(k, p, True)

    sums = scatter_blocks(A, me, QPARTS, fwd, line, r2, r3, ss_, sr, started, ready)
    total = jnp.concatenate([s[16 * c : 16 * c + 16] for s in sums for c in range(4)], axis=1) + resid[...].astype(F32)
    for z in range(4):
        rows = total[4 * z : 4 * z + 4]
        fout[z] = jnp.concatenate([rows[:, 384 * q : 384 * q + 384] for q in range(4)], axis=0).astype(BF16)
    outs = []
    for d in (2, 1, 3):
        c = remote(fout.at[turned(me["z"], d)], fin.at[me["z"]], fs.at[d - 1], fr.at[d - 1], device(me, z=d))
        c.start()
        outs.append(c)
    fin[me["z"]] = fout[me["z"]]
    for d in (1, 3, 2):
        there = fin.at[turned(me["z"], -d)]
        remote(there, there, fs.at[d - 1], fr.at[d - 1], device(me, k=1)).wait_recv()
    for c in outs:
        c.wait_send()
    for z in range(4):
        f = fin[z].astype(F32)
        rows = jnp.concatenate([f[4 * q : 4 * q + 4] for q in range(4)], axis=1).astype(BF16)
        o_ref[0, :, 1536 * z : 1536 * z + 1536] = rows[0:2]
        o_ref[1, :, 1536 * z : 1536 * z + 1536] = rows[2:4]


ANY = pl.BlockSpec(memory_space=pl.ANY)
VM = pl.BlockSpec(memory_space=pltpu.VMEM)
SM = pl.BlockSpec(memory_space=pltpu.SMEM)
DMA = pltpu.SemaphoreType.DMA


def on_device(hidden_in, queries, new_kv, kv_pool, block_table, cached_len, w_out, norm_gain, expert_ids, expert_gates,
              w_gate, w_up, w_down):
    V = pltpu.VMEM
    return pl.pallas_call(
        layer_kernel,
        out_shape=jax.ShapeDtypeStruct((2, 2, 6144), BF16),
        in_specs=[VM, SM, SM, SM, VM, VM, VM, VM] + [ANY] * 5,
        out_specs=VM,
        scratch_shapes=[
            V((4, 2, 4, 4, 208, 128), BF16), V((4, 2, 4, 4, 192, 128), BF16), V((32, 16, 2048), BF16), V((32, 128, 128), BF16),
            V((384, 6144), BF16), V((6144, 512), BF16), V((6144, 512), BF16), V((512, 6144), BF16),
            V((36, 128, 128), F32), V((36, 1, 128), F32), V((36, 1, 128), F32), V((40, 128), F32), V((40, 128), F32),
            V((36, 3, 64, 128), BF16), V((3, 36, 1, 128), F32), V((3, 36, 1, 128), F32), V((40, 128), jnp.int32), V((2, 256, 384), BF16),
            V((3, 2, 4, 2, 2, 8, 128), F32), V((3, 4, 2, 2, 8, 128), F32), V((4, 4, 4, 192, 128), BF16),
            V((3, 2, 2, 4, 64, 128), BF16), V((3, 2, 4, 2, 64, 128), BF16), V((3, 2, 4, 4, 64, 128), BF16),
            V((3, 3, 4, 64, 128), BF16), V((3, 3, 64, 128), BF16),
            V((3, 2, 2, 8, 128), F32), V((3, 2, 2, 2, 8, 128), F32), V((3, 4, 8, 128), F32), V((3, 3, 8, 128), F32), V((3, 4, 8, 128), F32), V((3, 3, 8, 128), F32),
            V((192, 128), F32), V((2, 16, 128), F32), V((2, 16, 128), F32), V((48, 128), F32),
            V((40, 256), jnp.int32), V((8, 256), jnp.int32), pltpu.SMEM((8, 256), jnp.int32),
            V((16, 16, 128), BF16), V((16, 16, 128), BF16),
            V((4, 4, 16, 1536), BF16), V((16, 16, 1536), BF16), V((16, 1536), F32), V((4, 16, 384), BF16), V((4, 16, 384), BF16),
            V((4, 2, 4, 16, 1024), F32), V((4, 2, 4, 16, 512), BF16), V((2, 4, 2, 4, 16, 128), F32), V((16, 1536), BF16),
            V((4, 16, 384), BF16), V((4, 16, 384), BF16),
            DMA((6,)), DMA((3, 12)), DMA((3, 12)), DMA((3, 4)), DMA((3, 4)), DMA((3, 12)), DMA((3, 12)), DMA((3, 12)), DMA((3, 12)),
            DMA((3,)), DMA((3,)), DMA((3,)), DMA((3,)), DMA((3,)), DMA((3,)), DMA((16,)), DMA((16,)), DMA((16,)), DMA((16,)),
            DMA((3, 12)), DMA((3, 12)), DMA((3, 4)), DMA((3, 4)), DMA((3, 12)), DMA((3, 12)), DMA((3,)), DMA((3,)), DMA((3,)), DMA((3,)),
        ],
        compiler_params=pltpu.CompilerParams(collective_id=0, has_side_effects=True, vmem_limit_bytes=63 * 2**20),
    )(block_table.T, cached_len, expert_ids, expert_gates, queries, new_kv, hidden_in, norm_gain.reshape(48, 128),
      kv_pool, w_out, w_gate, w_up, w_down)


def solution(mesh):
    both = ("row", "col")
    return jax.shard_map(
        on_device,
        mesh=mesh,
        in_specs=(P(both, None, None), P(both, None, None), P(both, None, None), P(both, None, None), P(), P(), P("col", None),
                  P(), P(both, None, None), P(both, None, None), P("row", None, "col"), P("row", None, "col"), P("row", "col", None)),
        out_specs=P(both, None, None),
        check_vma=False,
    )
```

```python
import jax, functools
import jax.numpy as jnp
from jax import lax
from jax.experimental import pallas as pl
from jax.experimental.pallas import tpu as pltpu
from jax.sharding import PartitionSpec as P

MESH = pl.DeviceIdType.MESH
ORDERS = (("x", "y", "z"), ("y", "z", "x"), ("z", "x", "y"))
F32, BF16 = jnp.float32, jnp.bfloat16


def where_am_i():
    r, c = lax.axis_index("row"), lax.axis_index("col")
    return {"y": lax.div(r, 2), "k": lax.rem(r, 2), "x": lax.div(c, 4), "z": lax.rem(c, 4)}


def turned(v, step):
    return lax.rem(v + (step + 4), 4)


def device(me, **moved):
    at = dict(me)
    for name, step in moved.items():
        at[name] = lax.rem(me[name] + step, 2) if name == "k" else turned(me[name], step)
    return (at["y"] * 2 + at["k"], at["x"] * 4 + at["z"])


def pick(sel, name):
    return sel.get(name, slice(None))


def block_of(ref, k, sel, part):
    return ref.at[(pick(sel, "y"), k, pick(sel, "x"), pick(sel, "z")) + part]


def remote(src, dst, send, recv, where):
    return pltpu.make_async_remote_copy(
        src_ref=src, dst_ref=dst, send_sem=send, recv_sem=recv, device_id=where, device_id_type=MESH
    )


def greet(me, plane=False):
    bar = pltpu.get_barrier_semaphore()
    count = 0
    for name in ("x", "y", "z"):
        for d in (1, 2, 3):
            pl.semaphore_signal(bar, inc=1, device_id=device(me, **{name: d}), device_id_type=MESH)
            count += 1
    pl.semaphore_signal(bar, inc=1, device_id=device(me, k=1), device_id_type=MESH)
    count += 1
    if plane:
        for dx in (1, 2, 3):
            for dz in (1, 2, 3):
                pl.semaphore_signal(bar, inc=1, device_id=device(me, x=dx, z=dz), device_id_type=MESH)
                count += 1
    pl.semaphore_wait(bar, count)


def shift(me, **moved):
    return {n: turned(me[n], -s) for n, s in moved.items()}


HALF = (slice(0, 2), slice(2, 4))


def gather_blocks(buf, me, parts, send, recv, cs, cr, hooks=(), on_line=None):
    k = me["k"]
    started = []

    def go(p, sel, moved, i):
        there = block_of(buf, k, sel, parts[p])
        copy = remote(there, there, send.at[p, i], recv.at[p, i], device(me, **moved))
        copy.start()
        started.append(copy)

    def landed(p, sel, i):
        here = block_of(buf, k, sel, parts[p])
        remote(here, here, send.at[p, i], recv.at[p, i], device(me, k=1)).wait_recv()

    def across(p, sel, i, kk=k):
        there = block_of(buf, kk, sel, parts[p])
        return remote(there, there, cs.at[p, i], cr.at[p, i], device(me, k=1))

    def cross(p, sel, i):
        copy = across(p, sel, i)
        copy.start()
        started.append(copy)

    for p, (a, b, c) in enumerate(ORDERS):
        for d in (2, 1, 3):
            go(p, {n: me[n] for n in "xyz"}, {a: d}, d - 1)
    if hooks:
        hooks[0]()
    for p, (a, b, c) in enumerate(ORDERS):
        for d in (1, 3, 2):
            landed(p, {a: turned(me[a], -d), b: me[b], c: me[c]}, d - 1)
        for d in (2, 1, 3):
            go(p, {b: me[b], c: me[c]}, {b: d}, 3 + d - 1)
    if hooks:
        hooks[1]()
    for p, (a, b, c) in enumerate(ORDERS):
        for d in (1, 3, 2):
            landed(p, {b: turned(me[b], -d), c: me[c]}, 3 + d - 1)
        go(p, {b: HALF[0], c: me[c]}, {c: 1}, 6)
        go(p, {b: HALF[1], c: me[c]}, {c: -1}, 9)
        go(p, {b: HALF[1], c: me[c]}, {c: 1}, 7)
        go(p, {b: HALF[0], c: me[c]}, {c: -1}, 8)
        cross(p, {c: me[c]}, 0)
    if hooks:
        hooks[2]()

    def both_cores(i, d):
        for p, (a, b, c) in enumerate(ORDERS):
            across(p, {c: turned(me[c], d)}, i, 1 - k).wait_recv()
        if on_line:
            on_line(d)

    both_cores(0, 0)
    for p, (a, b, c) in enumerate(ORDERS):
        landed(p, {b: HALF[0], c: turned(me[c], -1)}, 6)
        go(p, {b: HALF[0], c: turned(me[c], -1)}, {c: 1}, 10)
        landed(p, {b: HALF[1], c: turned(me[c], 1)}, 9)
        go(p, {b: HALF[1], c: turned(me[c], 1)}, {c: -1}, 11)
    for p, (a, b, c) in enumerate(ORDERS):
        landed(p, {b: HALF[1], c: turned(me[c], -1)}, 7)
        cross(p, {c: turned(me[c], -1)}, 1)
        landed(p, {b: HALF[0], c: turned(me[c], 1)}, 8)
        cross(p, {c: turned(me[c], 1)}, 2)
    both_cores(1, 3)
    both_cores(2, 1)
    for p, (a, b, c) in enumerate(ORDERS):
        landed(p, {b: HALF[0], c: turned(me[c], 2)}, 10)
        landed(p, {b: HALF[1], c: turned(me[c], 2)}, 11)
        cross(p, {c: turned(me[c], 2)}, 3)
    both_cores(3, 2)
    for copy in started:
        copy.wait_send()


def send_core(buf, me, parts, core, cs, cr, p):
    copy = remote(
        buf.at[(slice(None), 1 - me["k"], slice(None), slice(None)) + parts[p]],
        core.at[(slice(None), slice(None), slice(None)) + parts[p]],
        cs.at[p], cr.at[p], device(me, k=1),
    )
    copy.start()
    return copy


def scatter_blocks(buf, me, parts, fwd, line, r2, r3, send, recv, started, ready):
    k = me["k"]

    def go(p, sel, moved, dst, i):
        copy = remote(block_of(buf, k, sel, parts[p]), dst, send.at[p, i], recv.at[p, i], device(me, **moved))
        copy.start()
        started.append(copy)

    def landed(p, dst, i):
        remote(dst, dst, send.at[p, i], recv.at[p, i], device(me, k=1)).wait_recv()

    def rest_of(c):
        return [n for n in ("y", "x", "z") if n != c]

    def sub(ref, p, j, b, c, half):
        return ref.at[(p, j) + tuple(HALF[half] if n == b else slice(None) for n in rest_of(c))]

    def add(p, b, c, at, half, terms):
        rest = rest_of(c)

        for n in range(8):
            i_b, i_a = 2 * half + n // 4, n % 4
            idx = {c: at, **{m: (i_b if m == b else i_a) for m in rest}}
            mine = (idx["y"], k, idx["x"], idx["z"]) + parts[p]
            total = buf[mine].astype(F32)
            for t in terms:
                total += t(idx, rest, n).astype(F32)
            buf[mine] = total.astype(BF16)

    for p, (a, b, c) in enumerate(ORDERS):
        ready(p)
        far, right, left = turned(me[c], 2), turned(me[c], 1), turned(me[c], -1)
        go(p, {c: far, b: HALF[0]}, {c: 1}, fwd_dst(fwd, p, 0, a, b, c), 0)
        go(p, {c: far, b: HALF[1]}, {c: -1}, fwd_dst(fwd, p, 1, a, b, c), 1)
        go(p, {c: right, b: HALF[1]}, {c: 1}, sub(line, p, 0, b, c, 1), 2)
        go(p, {c: left, b: HALF[0]}, {c: -1}, sub(line, p, 1, b, c, 0), 3)
    for p, (a, b, c) in enumerate(ORDERS):
        right, left = turned(me[c], 1), turned(me[c], -1)
        landed(p, fwd_dst(fwd, p, 0, a, b, c), 0)
        add(p, b, c, right, 0, [fwd_at(fwd, p, 0, a, b, c)])
        go(p, {c: right, b: HALF[0]}, {c: 1}, sub(line, p, 0, b, c, 0), 4)
        landed(p, fwd_dst(fwd, p, 1, a, b, c), 1)
        add(p, b, c, left, 1, [fwd_at(fwd, p, 1, a, b, c)])
        go(p, {c: left, b: HALF[1]}, {c: -1}, sub(line, p, 1, b, c, 1), 5)
    for p, (a, b, c) in enumerate(ORDERS):
        for i, (j, h) in ((2, (0, 1)), (3, (1, 0)), (4, (0, 0)), (5, (1, 1))):
            landed(p, sub(line, p, j, b, c, h), i)
        def lt(j, p=p):
            return lambda idx, rest, n: line[p, j, idx[rest[0]], idx[rest[1]]]
        for h in range(2):
            add(p, b, c, me[c], h, [lt(0), lt(1)])
        for d in (2, 1, 3):
            go(p, {c: me[c], b: turned(me[b], d)}, {b: d}, r2.at[p, d - 1], 5 + d)
    for p, (a, b, c) in enumerate(ORDERS):
        for d in (1, 2, 3):
            landed(p, r2.at[p, d - 1], 5 + d)
        for i in range(4):
            idx = {c: me[c], b: me[b], a: i}
            mine = (idx["y"], k, idx["x"], idx["z"]) + parts[p]
            total = buf[mine].astype(F32)
            for d in range(3):
                total += r2[p, d, i].astype(F32)
            buf[mine] = total.astype(BF16)
        for d in (2, 1, 3):
            go(p, {c: me[c], b: me[b], a: turned(me[a], d)}, {a: d}, r3.at[p, d - 1], 8 + d)
    sums = []
    for p, (a, b, c) in enumerate(ORDERS):
        for d in (1, 2, 3):
            landed(p, r3.at[p, d - 1], 8 + d)
        total = buf[(me["y"], k, me["x"], me["z"]) + parts[p]].astype(F32)
        for d in range(3):
            total += r3[p, d].astype(F32)
        sums.append(total)
    for copy in started:
        copy.wait_send()
    return sums


def half_first(a, b, c):
    rest = [n for n in ("y", "x", "z") if n != c]
    return rest[0] == b


def fwd_dst(fwd, p, j, a, b, c):
    return fwd[half_first(a, b, c)].at[p, j]


def fwd_at(fwd, p, j, a, b, c):
    if half_first(a, b, c):
        return lambda idx, rest, n: fwd[True][p, j, n // 4, n % 4]
    return lambda idx, rest, n: fwd[False][p, j, n % 4, n // 4]


QPARTS = [(slice(64 * p, 64 * p + 64), slice(None)) for p in range(3)]
EMPTY = 34


def layer_kernel(table, clen, ids, gates, queries, new_kv, hidden, gain, kv_h, wo_h, wg_h, wu_h, wd_h, o_ref,
                 X, A, KV, VT, WO, WG, WU, WD, accs, ms, ls, ms2, ls2, Z, Zm, Zl, PI, PM, St, Cst, core, fa, fb, line, r2, r3, sf, sl, St2, s2, St3, s3,
                 U, NK, NV, GF, CC, info_v, info, G, H, O, Rv, hid, hin, hrec, acc, act, scal, resid, fout, fin,
                 lsem, gs, gr, gcs, gcr, ss_, sr, ts, tr, scs, scr, tcs, tcr, hs, hr, as_, ar, ps, pr,
                 gs2, gr2, gcs2, gcr2, ss2, sr2, scs2, scr2, fs, fr):
    me = where_am_i()
    k = me["k"]
    rank = me["y"] * 32 + k * 16 + me["x"] * 4 + me["z"]
    kv_load = pltpu.make_async_copy(kv_h, KV, lsem.at[0])
    wo_load = pltpu.make_async_copy(wo_h, WO, lsem.at[1])
    loads = [pltpu.make_async_copy(h.at[0], v, lsem.at[2 + i]) for i, (h, v) in enumerate(((wg_h, WG), (wu_h, WU), (wd_h, WD)))]
    info_load = pltpu.make_async_copy(info_v, info, lsem.at[5])
    kv_load.start()
    wo_load.start()
    for c in loads:
        c.start()
    for i in range(2):
        q = queries[i].astype(F32)
        for h in range(48):
            U[pl.ds((h // 16) * 64 + i * 32 + h % 16, 2, stride=16), :] = q[:, 128 * h : 128 * h + 128]
    X[me["y"], k, me["x"], me["z"], 0:192, :] = U[0:192, :].astype(BF16)
    greet(me, plane=True)
    started = []

    def find_blocks():
        code = lax.broadcasted_iota(jnp.int32, (64, 256), 1) * 64 + lax.broadcasted_iota(jnp.int32, (64, 256), 0)

        def search(j, _):
            CC[pl.ds(j, 1), :] = jnp.max(jnp.where(table[...] == rank * 32 + j, code, -1), axis=0, keepdims=True)
            return 0

        lax.fori_loop(0, 32, search, 0, unroll=4)
        CC[32:40, :] = jnp.full((8, 256), -1, jnp.int32)
        found = jnp.max(CC[...], axis=1, keepdims=True)
        r = lax.broadcasted_iota(jnp.int32, (40, 128), 0)
        c = lax.broadcasted_iota(jnp.int32, (40, 128), 1)
        found = jnp.broadcast_to(found, (40, 128))
        found = jnp.where((r == 32) | (r == 33), (rank * 2 + r - 32) * 64, found)
        owner = jnp.where(found >= 0, found // 64, -1)
        as_row = lambda v: jnp.max(jnp.where(r == c, v, -1), axis=0, keepdims=True)
        PI[...] = jnp.where(r == 35, 1, jnp.where(owner < 0, 0, owner % 2))
        owner_row, place_row = as_row(owner), as_row(jnp.where(found >= 0, found % 64, 0))
        before = jnp.max(jnp.where((owner == owner_row) & (r < c) & (owner >= 0), r, -1), axis=0, keepdims=True)
        info_v[1:2, 0:128] = jnp.where(before < 0, EMPTY, before)
        cr = c[0:1]
        info_v[2:3, 0:128] = jnp.where(cr < 34, jnp.maximum(owner_row, 0), jnp.where(cr == 35, 1, 0))
        info_v[3:4, 0:128] = jnp.maximum(place_row, 0)
        r2_ = lax.broadcasted_iota(jnp.int32, (40, 256), 0)
        c2_ = lax.broadcasted_iota(jnp.int32, (40, 256), 1)
        owner2 = jnp.concatenate([owner, owner], axis=1)
        last_ = jnp.max(jnp.where(owner2 == c2_, r2_, -1), axis=0, keepdims=True)
        info_v[0:1, :] = jnp.where(last_ < 0, EMPTY + c2_[0:1] % 2, last_)
        info_load.start()

    def small_things():
        for i in range(2):
            v = new_kv[i].astype(F32)
            for g in range(8):
                NK[i, 2 * g : 2 * g + 2, :] = v[:, 128 * g : 128 * g + 128]
                NV[i, 2 * g : 2 * g + 2, :] = v[:, 1024 + 128 * g : 1152 + 128 * g]
        GF[...] = gain[...].astype(F32)
        f = jnp.concatenate([hidden[0].astype(F32), hidden[1].astype(F32)], axis=0)
        for z in range(4):
            hin[z] = jnp.concatenate([f[:, 1536 * z + 384 * q : 1536 * z + 384 * q + 384] for q in range(4)], axis=0).astype(BF16)
        for d in (1, 2, 3):
            c = remote(hin.at[turned(me["z"], d)], hrec.at[me["z"]], hs.at[d - 1], hr.at[d - 1], device(me, z=d))
            c.start()
            started.append(c)
        hrec[me["z"]] = hin[me["z"]]

    def turn_values():
        kv_load.wait()

        def turn(j, _):
            v = jnp.concatenate([KV[j, :, 1024 + 128 * g : 1152 + 128 * g] for g in range(8)], axis=0)
            VT[j] = v.astype(F32).T.astype(BF16)
            return 0

        lax.fori_loop(0, 32, turn, 0, unroll=4)
        fresh_slots()

    lane = lax.broadcasted_iota(jnp.int32, (128, 128), 1)
    rowi = lax.broadcasted_iota(jnp.int32, (128, 128), 0)
    head_kv = jnp.where(lane < 96, ((lane // 32) * 16 + lane % 16) // 6, -1)
    lane_s = (lane // 16) % 2
    same = jnp.where(head_kv == rowi // 16, rowi % 16, 99)
    to_bits = 128 ** -0.5 * 1.4426950408889634

    def query_rows(at, i):
        first = jnp.broadcast_to(jnp.asarray(i, jnp.int32), (32, 128)) == 0
        pieces = []
        for p in (0, 1, 2):
            a, b = (X[at + (slice(64 * p + o, 64 * p + o + 32), slice(None))].astype(F32) for o in (0, 32))
            pieces.append(jnp.where(first, a, b).astype(BF16))
        return jnp.concatenate(pieces + pieces[:1], axis=0)

    def attend(st, ok, vt, j):
        st = jnp.where(ok, st, -1e30)
        m = jnp.max(st, axis=0, keepdims=True)
        w = jnp.exp2((st - m) * to_bits)
        accs[j] = jnp.dot(vt, w.astype(BF16), preferred_element_type=F32)
        ms[j] = m * to_bits
        ls[j] = jnp.sum(w, axis=0, keepdims=True)

    def fresh_slots():
        r = rowi[:16]
        for i in range(32, 36):
            ms[i] = jnp.full((1, 128), -1e30, F32)
            ls[i] = jnp.zeros((1, 128), F32)
        ms2[32:40, :] = jnp.full((8, 128), -1e30, F32)
        ls2[32:40, :] = jnp.zeros((8, 128), F32)
        row2 = lax.broadcasted_iota(jnp.int32, (256, 384), 0)
        col2 = lax.broadcasted_iota(jnp.int32, (256, 384), 1)
        source = (col2 % 128) // 64 * 128 + col2 // 128 * 32 + col2 % 32
        for i in range(2):
            PM[i] = jnp.where((row2 == source) & ((col2 // 32) % 2 == i), 1.0, 0.0).astype(BF16)
            own = query_rows((me["y"], k, me["x"], me["z"]), i)
            st = lax.dot_general(NK[i].astype(BF16), own, (((1,), (1,)), ((), ())), preferred_element_type=F32)
            attend(st, (head_kv[:16] == r // 2) & (r % 2 <= lane_s[:16]), NV[i].T.astype(BF16), 32 + i)
            accs[EMPTY + i] = jnp.zeros((128, 128), F32)

    gather_blocks(X, me, QPARTS, gs, gr, gcs, gcr, (find_blocks, small_things, turn_values))
    info_load.wait()

    def score(j, _):
        rq = info[2, j]
        q = query_rows((lax.div(rq, 64), lax.rem(lax.div(rq, 32), 2), lax.rem(lax.div(rq, 8), 4), lax.rem(lax.div(rq, 2), 4)), lax.rem(rq, 2))
        ks = jnp.concatenate([KV[j, :, 128 * g : 128 * g + 128] for g in range(8)], axis=0)
        accs[j] = lax.dot_general(ks, q, (((1,), (1,)), ((), ())), preferred_element_type=F32)
        return 0

    def weigh(j, _):
        seen = jnp.clip(clen[info[2, j]] - 16 * info[3, j], 0, 16)
        st = jnp.where(same < seen, accs[j], -1e30)
        m = jnp.max(st, axis=0, keepdims=True)
        w = jnp.exp2((st - m) * to_bits)
        ms[j] = m * to_bits
        ls[j] = jnp.sum(w, axis=0, keepdims=True)
        Z[j, 0] = w[:64].astype(BF16)
        Z[j, 1] = w[64:].astype(BF16)
        return 0

    def mix(j, _):
        accs[j] = jnp.dot(VT[j], jnp.concatenate([Z[j, 0], Z[j, 1]], axis=0), preferred_element_type=F32)
        return 0

    lax.fori_loop(0, 32, score, 0, unroll=8)
    lax.fori_loop(0, 32, weigh, 0, unroll=4)
    lax.fori_loop(0, 32, mix, 0, unroll=8)
    def chain(j, _):
        pj = info[1, j]
        m0, m1 = ms[j], ms[pj]
        m = jnp.maximum(m0, m1)
        w0, w1 = jnp.exp2(m0 - m), jnp.exp2(m1 - m)
        l = ls[j] * w0 + ls[pj] * w1
        accs[j] = accs[j] * w0 + accs[pj] * w1
        ls[j] = l
        ms[j] = m
        ms2[pl.ds(j, 1), :] = m
        ls2[pl.ds(j, 1), :] = l
        return 0

    def put(j, _):
        both = jnp.concatenate([accs[j, 0:64, :], accs[j, 64:128, :]], axis=1).astype(BF16)
        t = jnp.dot(both, PM[lax.rem(info[2, j], 2)], preferred_element_type=F32).astype(BF16)
        for p in range(3):
            Z[j, p] = t[:, 128 * p : 128 * p + 128]
        return 0

    lax.fori_loop(0, 34, chain, 0, unroll=2)
    lax.fori_loop(0, 36, put, 0, unroll=6)
    ln = lane[:40]
    for v, Zv in ((ms2, Zm), (ls2, Zl)):
        for p in range(3):
            t = jnp.where(ln < 64, pltpu.roll(v[...], (128 - 32 * p) % 128, 1), pltpu.roll(v[...], (192 - 32 * p) % 128, 1))
            t = jnp.where(ln % 64 < 32, t, 0.0)
            t = jnp.where(PI[...] == 0, t, pltpu.roll(t, 32, 1))
            for j in range(36):
                Zv[p, j] = t[j : j + 1]
    def spread(kk, ps_):
        def body(y, _):
            for x in range(4):
                for z in range(4):
                    to = y * 32 + kk * 16 + x * 4 + z
                    s0, s1_ = info[0, 2 * to], info[0, 2 * to + 1]
                    for p in ps_:
                        A[y, kk, x, z, 64 * p : 64 * p + 64, :] = Z[s0, p] + Z[s1_, p]
                        m, l = (Zv[p, s0] + Zv[p, s1_] for Zv in (Zm, Zl))
                        if p == 0:
                            at = (z, lax.div(y, 2), pl.ds(lax.rem(y, 2) * 4 + x, 1))
                        elif p == 1:
                            at = (x, z // 2, pl.ds((z % 2) * 4 + y, 1))
                        else:
                            at = (y, x // 2, slice((x % 2) * 4 + z, (x % 2) * 4 + z + 1))
                        St[(p, kk) + at[:2] + (0, at[2], slice(None))] = m
                        St[(p, kk) + at[:2] + (1, at[2], slice(None))] = l
            return 0

        lax.fori_loop(0, 4, body, 0)

    cores = []
    for p in range(3):
        spread(1 - k, (p,))
        c0 = send_core(A, me, QPARTS, core, scs, scr, p)
        c1 = remote(St.at[p, 1 - k], Cst.at[p], tcs.at[p], tcr.at[p], device(me, k=1))
        c1.start()
        cores.append((c0, c1))
        started.extend((c0, c1))
    spread(k, (0, 1, 2))

    def go(p, sel, moved, dst, i, stat, sdst):
        c0 = remote(block_of(A, k, sel, QPARTS[p]), dst, ss_.at[p, i], sr.at[p, i], device(me, **moved))
        c1 = remote(stat, sdst, ts.at[p, i], tr.at[p, i], device(me, **moved))
        c0.start()
        c1.start()
        started.extend((c0, c1))

    def landed(p, dst, i, sdst):
        remote(dst, dst, ss_.at[p, i], sr.at[p, i], device(me, k=1)).wait_recv()
        remote(sdst, sdst, ts.at[p, i], tr.at[p, i], device(me, k=1)).wait_recv()

    def merge(stats):
        top = functools.reduce(jnp.maximum, [m for m, _ in stats])
        ws = [jnp.exp2(m - top) for m, _ in stats]
        return top, sum(w * l for w, (_, l) in zip(ws, stats)), ws

    def others(c):
        return [n for n in ("y", "x", "z") if n != c]

    fwd = {True: fa, False: fb}

    def half_line(p, j, b, c, h):
        return line.at[(p, j) + tuple(HALF[h] if n == b else slice(None) for n in others(c))]

    def blend(p, at, h, sources):
        a, b, c = ORDERS[p]
        here = St[p, k, at, h]
        stats = [(here[0], here[1])] + [(s[0], s[1]) for _, s in sources]
        top, tot, ws = merge(stats)
        St[p, k, at, h, 0] = top
        St[p, k, at, h, 1] = tot
        for n in range(8):
            idx = {c: at, b: 2 * h + n // 4, a: n % 4}
            mine = (idx["y"], k, idx["x"], idx["z"]) + QPARTS[p]
            t = A[mine].astype(F32) * ws[0][n : n + 1]
            for i, (block, _) in enumerate(sources):
                t += block(idx, n).astype(F32) * ws[i + 1][n : n + 1]
            A[mine] = t.astype(BF16)

    def from_core(p, at, h):
        return (lambda idx, n: core[(idx["y"], idx["x"], idx["z"]) + QPARTS[p]]), Cst[p, at, h]

    def from_fwd(p, j):
        a, b, c = ORDERS[p]
        get = fwd_at(fwd, p, j, a, b, c)
        return (lambda idx, n: get(idx, None, n)), sf[p, j]

    def from_line(p, j, h):
        rest = others(ORDERS[p][2])
        return (lambda idx, n: line[p, j, idx[rest[0]], idx[rest[1]]]), sl[p, j, h]

    for p, (a, b, c) in enumerate(ORDERS):
        for copy in cores[p]:
            copy.wait_recv()
        far, right, left = turned(me[c], 2), turned(me[c], 1), turned(me[c], -1)
        blend(p, far, 0, [from_core(p, far, 0)])
        go(p, {c: far, b: HALF[0]}, {c: 1}, fwd_dst(fwd, p, 0, a, b, c), 0, St.at[p, k, far, 0], sf.at[p, 0])
        blend(p, far, 1, [from_core(p, far, 1)])
        go(p, {c: far, b: HALF[1]}, {c: -1}, fwd_dst(fwd, p, 1, a, b, c), 1, St.at[p, k, far, 1], sf.at[p, 1])
        blend(p, right, 1, [from_core(p, right, 1)])
        go(p, {c: right, b: HALF[1]}, {c: 1}, half_line(p, 0, b, c, 1), 2, St.at[p, k, right, 1], sl.at[p, 0, 1])
        blend(p, left, 0, [from_core(p, left, 0)])
        go(p, {c: left, b: HALF[0]}, {c: -1}, half_line(p, 1, b, c, 0), 3, St.at[p, k, left, 0], sl.at[p, 1, 0])
    for p, (a, b, c) in enumerate(ORDERS):
        right, left = turned(me[c], 1), turned(me[c], -1)
        landed(p, fwd_dst(fwd, p, 0, a, b, c), 0, sf.at[p, 0])
        blend(p, right, 0, [from_core(p, right, 0), from_fwd(p, 0)])
        go(p, {c: right, b: HALF[0]}, {c: 1}, half_line(p, 0, b, c, 0), 4, St.at[p, k, right, 0], sl.at[p, 0, 0])
        landed(p, fwd_dst(fwd, p, 1, a, b, c), 1, sf.at[p, 1])
        blend(p, left, 1, [from_core(p, left, 1), from_fwd(p, 1)])
        go(p, {c: left, b: HALF[1]}, {c: -1}, half_line(p, 1, b, c, 1), 5, St.at[p, k, left, 1], sl.at[p, 1, 1])
    for p, (a, b, c) in enumerate(ORDERS):
        for h in range(2):
            blend(p, me[c], h, [from_core(p, me[c], h)])
    for p, (a, b, c) in enumerate(ORDERS):
        for i, (j, h) in ((2, (0, 1)), (3, (1, 0)), (4, (0, 0)), (5, (1, 1))):
            landed(p, half_line(p, j, b, c, h), i, sl.at[p, j, h])
        for h in range(2):
            blend(p, me[c], h, [from_line(p, 0, h), from_line(p, 1, h)])
            for i in range(2):
                St2[p, 2 * h + i, 0:4] = St[p, k, me[c], h, 0, 4 * i : 4 * i + 4]
                St2[p, 2 * h + i, 4:8] = St[p, k, me[c], h, 1, 4 * i : 4 * i + 4]
        for d in (2, 1, 3):
            at = turned(me[b], d)
            go(p, {c: me[c], b: at}, {b: d}, r2.at[p, d - 1], 5 + d, St2.at[p, at], s2.at[p, d - 1])
    for p, (a, b, c) in enumerate(ORDERS):
        for d in (1, 2, 3):
            landed(p, r2.at[p, d - 1], 5 + d, s2.at[p, d - 1])
        stats = [St2[p, me[b]]] + [s2[p, d] for d in range(3)]
        top, tot, ws = merge([(s[0:4], s[4:8]) for s in stats])
        for i in range(4):
            idx = {c: me[c], b: me[b], a: i}
            mine = (idx["y"], k, idx["x"], idx["z"]) + QPARTS[p]
            t = A[mine].astype(F32) * ws[0][i : i + 1]
            for d in range(3):
                t += r2[p, d, i].astype(F32) * ws[d + 1][i : i + 1]
            A[mine] = t.astype(BF16)
            St3[p, i, 0:1] = top[i : i + 1]
            St3[p, i, 1:2] = tot[i : i + 1]
        for d in (2, 1, 3):
            at = turned(me[a], d)
            go(p, {c: me[c], b: me[b], a: at}, {a: d}, r3.at[p, d - 1], 8 + d, St3.at[p, at], s3.at[p, d - 1])
    for p, (a, b, c) in enumerate(ORDERS):
        for d in (1, 2, 3):
            landed(p, r3.at[p, d - 1], 8 + d, s3.at[p, d - 1])
        stats = [St3[p, me[a]]] + [s3[p, d] for d in range(3)]
        top, tot, ws = merge([(s[0:1], s[1:2]) for s in stats])
        t = A[(me["y"], k, me["x"], me["z"]) + QPARTS[p]].astype(F32) * ws[0]
        for d in range(3):
            t += r3[p, d].astype(F32) * ws[d + 1]
        t = t / tot
        both = jnp.concatenate([t, pltpu.roll(t, 64, 1)], axis=0)
        U[64 * p : 64 * p + 64, :] = both.T[:64]
    for c in range(16):
        rows = []
        for hh in range(3):
            h = 3 * c + hh
            rows.append(U[pl.ds((h // 16) * 64 + h % 16, 4, stride=16), :])
        G[c] = jnp.concatenate(rows + [jnp.zeros((4, 128), F32)], axis=0).astype(BF16)
    col = me["x"] * 4 + me["z"]
    steps = [(dx, dz) for dz in (2, 1, 3, 0) for dx in (2, 1, 3, 0) if dx or dz]

    def peer(dx, dz):
        return (turned(me["x"], dx)) * 4 + turned(me["z"], dz)

    for dx, dz in steps:
        c = remote(G.at[peer(dx, dz)], H.at[col], as_.at[dx * 4 + dz], ar.at[dx * 4 + dz], device(me, x=dx, z=dz))
        c.start()
        started.append(c)
    H[col] = G[col]
    for d in (1, 2, 3):
        there = hrec.at[turned(me["z"], -d)]
        remote(there, there, hs.at[d - 1], hr.at[d - 1], device(me, k=1)).wait_recv()
    for z in range(4):
        f = hrec[z].astype(F32)
        hid[4 * z : 4 * z + 4, :] = jnp.concatenate([f[4 * q : 4 * q + 4] for q in range(4)], axis=1)
    wo_load.wait()
    for dx, dz in steps:
        there = H.at[peer(-dx, -dz)]
        remote(there, there, as_.at[dx * 4 + dz], ar.at[dx * 4 + dz], device(me, k=1)).wait_recv()
    heads = []
    hf = [H[c].astype(F32) for c in range(16)]
    for hh in range(3):
        heads.append(jnp.concatenate([hf[c][4 * hh : 4 * hh + 4] for c in range(16)], axis=0).astype(BF16))
    lhs = jnp.concatenate(heads, axis=1)
    for dz in (2, 1, 3, 0):
        zz = turned(me["z"], dz)
        res = jnp.dot(lhs, WO[:, pl.ds(pl.multiple_of(zz * 1536, 1536), 1536)], preferred_element_type=F32).astype(BF16)
        for x in range(4):
            O[x, zz] = res[16 * x : 16 * x + 16]
        for dx in (2, 1, 3, 0):
            if dx or dz:
                c = remote(O.at[turned(me["x"], dx), zz], Rv.at[col], ps.at[dx * 4 + dz], pr.at[dx * 4 + dz], device(me, x=dx, z=dz))
                c.start()
                started.append(c)
    Rv[col] = O[me["x"], me["z"]]
    for dx, dz in steps:
        there = Rv.at[peer(-dx, -dz)]
        remote(there, there, ps.at[dx * 4 + dz], pr.at[dx * 4 + dz], device(me, k=1)).wait_recv()
    total = Rv[0].astype(F32)
    for c in range(1, 16):
        total += Rv[c].astype(F32)
    res = (hid[...] + total).astype(BF16)
    resid[...] = res
    f = res.astype(F32)
    xg = jnp.concatenate([f[:, 128 * c : 128 * c + 128] * GF[pl.ds(me["z"] * 12 + c, 1), :] for c in range(12)], axis=1).astype(BF16)
    squares = jnp.sum(f * f, axis=1, keepdims=True)
    high = squares.astype(BF16).astype(F32)
    low = squares - high
    ln = lax.broadcasted_iota(jnp.int32, (16, 128), 1)
    rw = lax.broadcasted_iota(jnp.int32, (16, 128), 0)
    gt = jnp.zeros((16, 128), F32)
    for t in range(4):
        for n in range(2):
            gt += jnp.where((rw == 4 * me["z"] + t) & (ln == 8 + ids[t // 2, t % 2, n]), gates[t // 2, t % 2, n], 0.0)
    gh = gt.astype(BF16).astype(F32)
    tile = gh + pltpu.roll(gt - gh, 8, 1)
    tile = jnp.where(ln == 0, high, jnp.where(ln == 1, low, tile)).astype(BF16)
    here = (me["y"], k, me["x"], me["z"])
    for c in range(12):
        X[here + (slice(16 * c, 16 * c + 16), slice(None))] = xg[:, 128 * c : 128 * c + 128]
    X[here + (slice(192, 208), slice(None))] = tile
    for c in started:
        c.wait_send()
    experts(me, X, WG, WU, WD, A, core, fwd, line, r2, r3, acc, act, scal, resid, fout, fin, loads,
            gs2, gr2, gcs2, gcr2, ss2, sr2, scs2, scr2, fs, fr, o_ref)


XPARTS = [(slice(0, 64), slice(None)), (slice(64, 128), slice(None)), (slice(128, 208), slice(None))]


def experts(me, X, WG, WU, WD, A, core, fwd, line, r2, r3, acc, act, scal, resid, fout, fin, loads,
            gs, gr, gcs, gcr, ss_, sr, scs, scr, fs, fr, o_ref):
    k = me["k"]
    expert = me["y"] * 2 + k
    acc[...] = jnp.zeros_like(acc)

    def add_products(at, terms):
        xs = []
        for rows, z, p in terms:
            x = jnp.concatenate([X[rows + (slice(16 * n, 16 * n + 16), slice(None))] for n in range(4 * p, 4 * p + 4)], axis=-1)
            lead = x.shape[:-1]
            xs.append((x.reshape(-1, 512), pl.ds(pl.multiple_of(z * 1536 + 512 * p, 512), 512)))
        for n, W in enumerate((WG, WU)):
            for h in range(2):
                cols = slice(512 * n + 256 * h, 512 * n + 256 * h + 256)
                r = sum(jnp.dot(x, W[depth, 256 * h : 256 * h + 256], preferred_element_type=F32) for x, depth in xs)
                acc[at + (cols,)] += r.reshape(lead + (256,))

    def on_line(d):
        if d == 0:
            loads[0].wait()
            loads[1].wait()
        full = slice(None)
        z, x, y = turned(me["z"], d), turned(me["x"], d), turned(me["y"], d)
        add_products((full, full, full, full), [((full, full, full, z), z, 0)])
        add_products((full, full, x, full), [((full, full, x, zz), zz, 1) for zz in range(4)])
        add_products((y, full, full, full), [((y, full, full, zz), zz, 2) for zz in range(4)])

    gather_blocks(X, me, XPARTS, gs, gr, gcs, gcr, (), on_line)
    loads[2].wait()
    extra = jnp.zeros((512, 128), F32)
    for z in range(4):
        extra += X[:, :, :, z, 192:208, :].reshape(512, 128).astype(F32)
    lane = lax.broadcasted_iota(jnp.int32, (512, 128), 1)
    squares = jnp.sum(jnp.where(lane < 3, extra, 0.0), axis=1, keepdims=True)
    weight = jnp.sum(jnp.where((lane == 8 + expert) | (lane == 16 + expert), extra, 0.0), axis=1, keepdims=True)
    scal[0] = jnp.broadcast_to(lax.rsqrt(squares * (1.0 / 6144.0) + 1e-5), (512, 128)).reshape(4, 2, 4, 16, 128)
    scal[1] = jnp.broadcast_to(weight, (512, 128)).reshape(4, 2, 4, 16, 128)
    started = []

    def activate(kk):
        at = (slice(None), kk, slice(None), slice(None))
        for n in range(4):
            rs = scal[(0,) + at].reshape(256, 128)
            g = acc[at + (slice(128 * n, 128 * n + 128),)].reshape(256, 128) * rs
            u = acc[at + (slice(512 + 128 * n, 640 + 128 * n),)].reshape(256, 128) * rs
            v = g / (1.0 + jnp.exp(-g)) * u * scal[(1,) + at].reshape(256, 128)
            act[at + (slice(128 * n, 128 * n + 128),)] = v.astype(BF16).reshape(4, 4, 16, 128)

    def down(kk, p, with_core):
        def body(z, _):
            cols = pl.ds(pl.multiple_of(z * 1536 + 512 * p, 512), 512)
            r = jnp.dot(act[:, kk].reshape(256, 512), WD[:, cols], preferred_element_type=F32)
            for n in range(4):
                rows = slice(64 * p + 16 * n, 64 * p + 16 * n + 16)
                t = r[:, 128 * n : 128 * n + 128].reshape(4, 4, 16, 128)
                if with_core:
                    t += core[:, :, z, rows, :].astype(F32)
                A[:, kk, :, z, rows, :] = t.astype(BF16)
            return 0

        lax.fori_loop(0, 4, body, 0)

    activate(1 - k)
    for p in range(3):
        down(1 - k, p, False)
        started.append(send_core(A, me, QPARTS, core, scs, scr, p))
    activate(k)

    def ready(p):
        started[p].wait_recv()
        down(k, p, True)

    sums = scatter_blocks(A, me, QPARTS, fwd, line, r2, r3, ss_, sr, started, ready)
    total = jnp.concatenate([s[16 * c : 16 * c + 16] for s in sums for c in range(4)], axis=1) + resid[...].astype(F32)
    for z in range(4):
        rows = total[4 * z : 4 * z + 4]
        fout[z] = jnp.concatenate([rows[:, 384 * q : 384 * q + 384] for q in range(4)], axis=0).astype(BF16)
    outs = []
    for d in (2, 1, 3):
        c = remote(fout.at[turned(me["z"], d)], fin.at[me["z"]], fs.at[d - 1], fr.at[d - 1], device(me, z=d))
        c.start()
        outs.append(c)
    fin[me["z"]] = fout[me["z"]]
    for d in (1, 3, 2):
        there = fin.at[turned(me["z"], -d)]
        remote(there, there, fs.at[d - 1], fr.at[d - 1], device(me, k=1)).wait_recv()
    for c in outs:
        c.wait_send()
    for z in range(4):
        f = fin[z].astype(F32)
        rows = jnp.concatenate([f[4 * q : 4 * q + 4] for q in range(4)], axis=1).astype(BF16)
        o_ref[0, :, 1536 * z : 1536 * z + 1536] = rows[0:2]
        o_ref[1, :, 1536 * z : 1536 * z + 1536] = rows[2:4]


ANY = pl.BlockSpec(memory_space=pl.ANY)
VM = pl.BlockSpec(memory_space=pltpu.VMEM)
SM = pl.BlockSpec(memory_space=pltpu.SMEM)
DMA = pltpu.SemaphoreType.DMA


def on_device(hidden_in, queries, new_kv, kv_pool, block_table, cached_len, w_out, norm_gain, expert_ids, expert_gates,
              w_gate, w_up, w_down):
    V = pltpu.VMEM
    return pl.pallas_call(
        layer_kernel,
        out_shape=jax.ShapeDtypeStruct((2, 2, 6144), BF16),
        in_specs=[VM, SM, SM, SM, VM, VM, VM, VM] + [ANY] * 5,
        out_specs=VM,
        scratch_shapes=[
            V((4, 2, 4, 4, 208, 128), BF16), V((4, 2, 4, 4, 192, 128), BF16), V((32, 16, 2048), BF16), V((32, 128, 128), BF16),
            V((384, 6144), BF16), V((6144, 512), BF16), V((6144, 512), BF16), V((512, 6144), BF16),
            V((36, 128, 128), F32), V((36, 1, 128), F32), V((36, 1, 128), F32), V((40, 128), F32), V((40, 128), F32),
            V((36, 3, 64, 128), BF16), V((3, 36, 1, 128), F32), V((3, 36, 1, 128), F32), V((40, 128), jnp.int32), V((2, 256, 384), BF16),
            V((3, 2, 4, 2, 2, 8, 128), F32), V((3, 4, 2, 2, 8, 128), F32), V((4, 4, 4, 192, 128), BF16),
            V((3, 2, 2, 4, 64, 128), BF16), V((3, 2, 4, 2, 64, 128), BF16), V((3, 2, 4, 4, 64, 128), BF16),
            V((3, 3, 4, 64, 128), BF16), V((3, 3, 64, 128), BF16),
            V((3, 2, 2, 8, 128), F32), V((3, 2, 2, 2, 8, 128), F32), V((3, 4, 8, 128), F32), V((3, 3, 8, 128), F32), V((3, 4, 8, 128), F32), V((3, 3, 8, 128), F32),
            V((256, 128), F32), V((2, 16, 128), F32), V((2, 16, 128), F32), V((48, 128), F32),
            V((40, 256), jnp.int32), V((8, 256), jnp.int32), pltpu.SMEM((8, 256), jnp.int32),
            V((16, 16, 128), BF16), V((16, 16, 128), BF16),
            V((4, 4, 16, 1536), BF16), V((16, 16, 1536), BF16), V((16, 1536), F32), V((4, 16, 384), BF16), V((4, 16, 384), BF16),
            V((4, 2, 4, 16, 1024), F32), V((4, 2, 4, 16, 512), BF16), V((2, 4, 2, 4, 16, 128), F32), V((16, 1536), BF16),
            V((4, 16, 384), BF16), V((4, 16, 384), BF16),
            DMA((6,)), DMA((3, 12)), DMA((3, 12)), DMA((3, 4)), DMA((3, 4)), DMA((3, 12)), DMA((3, 12)), DMA((3, 12)), DMA((3, 12)),
            DMA((3,)), DMA((3,)), DMA((3,)), DMA((3,)), DMA((3,)), DMA((3,)), DMA((16,)), DMA((16,)), DMA((16,)), DMA((16,)),
            DMA((3, 12)), DMA((3, 12)), DMA((3, 4)), DMA((3, 4)), DMA((3, 12)), DMA((3, 12)), DMA((3,)), DMA((3,)), DMA((3,)), DMA((3,)),
        ],
        compiler_params=pltpu.CompilerParams(collective_id=0, has_side_effects=True, vmem_limit_bytes=63 * 2**20),
    )(block_table.T, cached_len, expert_ids, expert_gates, queries, new_kv, hidden_in, norm_gain.reshape(48, 128),
      kv_pool, w_out, w_gate, w_up, w_down)


def solution(mesh):
    both = ("row", "col")
    return jax.shard_map(
        on_device,
        mesh=mesh,
        in_specs=(P(both, None, None), P(both, None, None), P(both, None, None), P(both, None, None), P(), P(), P("col", None),
                  P(), P(both, None, None), P(both, None, None), P("row", None, "col"), P("row", None, "col"), P("row", "col", None)),
        out_specs=P(both, None, None),
        check_vma=False,
    )
```
